32 devices in a mesh: tm: 2 (over x), lon: 16 (over z, y, core).
Axes of the slice: x: 2, y: 2, z: 4, core: 2. Of those that a mesh axis runs over, the one named last changes fastest.
Arguments:
- snapshots: bfloat16 [2048, 128, 256], P('lon', 'tm'), may hold values from -6 to 6
- test_matrix: float32 [128, 64], replicated, may hold values from -6 to 6
Outputs:
- pod_modes: float32 [64, 327680], P(None, ('lon', 'tm'))
The draws below stay inside these ranges and needn't reach their ends.
All inputs are finite; a program needn't handle non-finite values.
Results may differ from the reference program's by a relative error of at most 0.0003.
Values may be sent and summed in bfloat16 or wider, within the bound.
No kernel may reach another device: no remote copies, remote signals or barrier semaphores. Data moves between devices by JAX's collectives and lax.ppermute only.
A program may use at most 128 MiB of HBM per device.

```python
import math
import jax
import jax.numpy as jnp
from jax import lax

RANK = 64
NPH = 2048
MMAX = 640
NTH = 256
TOTAL = 128
N_TM = 2


def block_scale(own_key, dims, cuts, least, high):
    def one(position, blocks):
        draws = jax.random.uniform(jax.random.fold_in(jax.random.fold_in(own_key, 6), position), (blocks,), jnp.float32, least / len(cuts), high / len(cuts))
        return jnp.repeat(jnp.exp(draws), dims[position] // blocks).reshape((-1,) + (1,) * (len(dims) - position - 1))

    loudness = one(*cuts[0])
    for cut in cuts[1:]:
        loudness = loudness * one(*cut)
    return loudness


def noise(own_key, extent, scale, reach, cuts=(), held_as=jnp.bfloat16):
    gain = block_scale(own_key, extent, cuts, -0.22, 0.18) if cuts else 1.0
    drawn = jax.random.normal(own_key, extent, jnp.float32) * scale * gain
    return jnp.minimum(jnp.maximum(drawn, -reach), reach).astype(held_as)


def setup_inputs(seed: int = 0) -> dict:
    arg_keys = jax.random.split(jax.random.key(seed), 3)
    snapshots = noise(arg_keys[0], (NPH, TOTAL, NTH), 1.0, 6.0, ((0, 16), (1, 2)))
    test_matrix = noise(arg_keys[1], (2 * RANK, RANK), 1.0, 6.0, (), jnp.float32)
    return {"snapshots": snapshots, "test_matrix": test_matrix}


highest = lax.Precision.HIGHEST

def matmul(first_op, second_op):
    return jnp.dot(first_op.astype(jnp.float32), second_op.astype(jnp.float32), precision=highest, preferred_element_type=jnp.float32)

def spectral_table(points, wave_count):
    lon_ids = jnp.arange(points, dtype=jnp.int32)
    col_ids = jnp.arange(2 * wave_count, dtype=jnp.int32)
    wavenumber = jnp.where(col_ids < wave_count, col_ids, col_ids - wave_count + 1)
    phase_index = lon_ids[:, None] * wavenumber[None, :] % points
    angles = 2.0 * math.pi / points * phase_index.astype(jnp.float32)
    trig_value = jnp.where(col_ids[None, :] < wave_count, jnp.cos(angles), jnp.sin(angles))
    col_scale = math.sqrt(2.0 / points) / jnp.sqrt(1.0 + 4.0 * wavenumber.astype(jnp.float32) / wave_count)
    return trig_value * col_scale[None, :]

def area_weight(start_row, row_count, total_rows):
    row_ids = start_row + jnp.arange(row_count, dtype=jnp.int32)
    colatitude = math.pi * (row_ids.astype(jnp.float32) + 0.5) / (2.0 * total_rows)
    return jnp.sqrt(jnp.sin(colatitude))

def merge_gram(gram_matrix, test_matrix):
    sketch = matmul(gram_matrix, test_matrix)
    sketch_gram = matmul(sketch.T, gram_matrix)
    power_gram = matmul(sketch_gram, sketch)
    power_gram = 0.5 * (power_gram + power_gram.T)
    chol_first = jnp.linalg.cholesky(power_gram)
    projected = lax.linalg.triangular_solve(chol_first, sketch_gram, left_side=True, lower=True)
    proj_gram = matmul(projected, projected.T)
    chol_second = jnp.linalg.cholesky(0.5 * (proj_gram + proj_gram.T))
    unmixed = lax.linalg.triangular_solve(chol_first, sketch.T, left_side=True, lower=True)
    mixing = matmul(chol_second.T, unmixed)
    return (mixing, matmul(chol_second.T, chol_second))

def block_gram(low_energy, cross_term, high_energy):
    top_rows = jnp.concatenate([low_energy, cross_term], axis=1)
    bottom_rows = jnp.concatenate([cross_term.T, high_energy], axis=1)
    return jnp.concatenate([top_rows, bottom_rows], axis=0)

def reference(snapshots, test_matrix):
    dft_table = spectral_table(NPH, MMAX)
    row_weight = area_weight(0, NTH, NTH)
    grouped = snapshots.reshape(NPH, N_TM, RANK, NTH).transpose(1, 0, 2, 3)

    def transform(slab_part):
        spectra = jnp.einsum('pst,pk->stk', slab_part.astype(jnp.float32), dft_table, precision=highest)
        return (spectra * row_weight[None, :, None]).reshape(RANK, NTH * 2 * MMAX)
    all_spectra = lax.map(transform, grouped)
    level_modes = [all_spectra[group_id] for group_id in range(N_TM)]
    level_energy = [matmul(modes_now, modes_now.T) for modes_now in level_modes]
    while len(level_modes) > 1:
        next_modes = []
        next_energy = []
        for pair_index in range(0, len(level_modes), 2):
            low_modes = level_modes[pair_index]
            high_modes = level_modes[pair_index + 1]
            cross_term = matmul(low_modes, high_modes.T)
            gram_matrix = block_gram(level_energy[pair_index], cross_term, level_energy[pair_index + 1])
            mixing, energy = merge_gram(gram_matrix, test_matrix)
            stacked = jnp.concatenate([low_modes, high_modes], axis=0)
            next_modes.append(matmul(mixing, stacked))
            next_energy.append(energy)
        level_modes = next_modes
        level_energy = next_energy
    return level_modes[0]
```

```python
import functools
import math

import jax
import jax.numpy as jnp
from jax import lax
from jax.experimental import pallas as pl
from jax.experimental.pallas import tpu as pltpu
from jax.sharding import PartitionSpec as P

NPH = 2048
MMAX = 640
NTH = 256
COL_TILE = 256


highest = lax.Precision.HIGHEST
NT_DIMS = (((1,), (1,)), ((), ()))


def swapped(array, axis, distance):
    return lax.ppermute(array, axis, [(i, i ^ 1 << distance) for i in range(lax.axis_size(axis))])


def matmul(first_op, second_op):
    return jnp.dot(first_op, second_op, precision=highest, preferred_element_type=jnp.float32)


def spectral_table(points, wave_count):
    lon_ids = jnp.arange(points, dtype=jnp.int32)
    col_ids = jnp.arange(2 * wave_count, dtype=jnp.int32)
    wavenumber = jnp.where(col_ids < wave_count, col_ids, col_ids - wave_count + 1)
    phase_index = lon_ids[:, None] * wavenumber[None, :] % points
    angles = 2.0 * math.pi / points * phase_index.astype(jnp.float32)
    trig_value = jnp.where(col_ids[None, :] < wave_count, jnp.cos(angles), jnp.sin(angles))
    col_scale = math.sqrt(2.0 / points) / jnp.sqrt(
        1.0 + 4.0 * wavenumber.astype(jnp.float32) / wave_count
    )
    return trig_value * col_scale[None, :]


def area_weight(start_row, row_count, total_rows):
    row_ids = start_row + jnp.arange(row_count, dtype=jnp.int32)
    colatitude = math.pi * (row_ids.astype(jnp.float32) + 0.5) / (2.0 * total_rows)
    return jnp.sqrt(jnp.sin(colatitude))


def merge_gram(gram_matrix, test_matrix):
    sketch = matmul(gram_matrix, test_matrix)
    sketch_gram = matmul(sketch.T, gram_matrix)
    power_gram = matmul(sketch_gram, sketch)
    power_gram = 0.5 * (power_gram + power_gram.T)
    chol_first = jnp.linalg.cholesky(power_gram)
    projected = lax.linalg.triangular_solve(chol_first, sketch_gram, left_side=True, lower=True)
    proj_gram = matmul(projected, projected.T)
    chol_second = jnp.linalg.cholesky(0.5 * (proj_gram + proj_gram.T))
    unmixed = lax.linalg.triangular_solve(chol_first, sketch.T, left_side=True, lower=True)
    mixing = matmul(chol_second.T, unmixed)
    return (mixing, matmul(chol_second.T, chol_second))


def block_gram(low_energy, cross_term, high_energy):
    top_rows = jnp.concatenate([low_energy, cross_term], axis=1)
    bottom_rows = jnp.concatenate([cross_term.T, high_energy], axis=1)
    return jnp.concatenate([top_rows, bottom_rows], axis=0)


def combine_pair(mixing, low_modes, high_modes):
    rank_rows = low_modes.shape[0]
    return matmul(mixing[:, :rank_rows], low_modes) + matmul(mixing[:, rank_rows:], high_modes)


def own_columns(modes_flat, group_index, group_count):
    col_count = modes_flat.shape[1] // group_count
    return lax.dynamic_slice_in_dim(modes_flat, group_index * col_count, col_count, 1)


def local_tree(snapshots, test_matrix):
    dev_rows = NTH // lax.axis_size("lon")
    dft_table = spectral_table(NPH, MMAX)
    row_weight = area_weight(lax.axis_index("lon") * dev_rows, dev_rows, NTH)
    spectra = jnp.einsum(
        "pst,pk->stk",
        lax.all_to_all(snapshots, "lon", split_axis=2, concat_axis=0, tiled=True).astype(
            jnp.float32
        ),
        dft_table,
        precision=highest,
    )
    spectra = spectra * row_weight[None, :, None]
    rank_rows = spectra.shape[0]
    modes_now = spectra.reshape(rank_rows, -1)
    levels_count = lax.axis_size("tm").bit_length() - 1
    group_index = lax.axis_index("tm")
    group_count = lax.axis_size("tm")
    energy = lax.psum(matmul(modes_now, modes_now.T), "lon")
    start_level = 0
    for tree_level in range(start_level, levels_count):
        partner_modes, partner_energy = swapped((modes_now, energy), "tm", tree_level)
        is_upper = group_index // 2**tree_level % 2 == 1
        low_modes = jnp.where(is_upper, partner_modes, modes_now)
        high_modes = jnp.where(is_upper, modes_now, partner_modes)
        low_energy = jnp.where(is_upper, partner_energy, energy)
        high_energy = jnp.where(is_upper, energy, partner_energy)
        cross_term = lax.psum(matmul(low_modes, high_modes.T), "lon")
        mixing, energy = merge_gram(block_gram(low_energy, cross_term, high_energy), test_matrix)
        modes_now = combine_pair(mixing, low_modes, high_modes)
    return own_columns(modes_now, group_index, group_count)


def split_table(points, wave_count):
    table = spectral_table(points, wave_count)
    high = lax.reduce_precision(table, 8, 7)
    return high.astype(jnp.bfloat16), (table - high).astype(jnp.bfloat16)


def spectra_kernel(weight_ref, x_ref, high_ref, low_ref, xh_ref, xl_ref, gram_ref, lhs, acc):
    sources, groups, rows, rank_rows, points = x_ref.shape
    step = pl.program_id(0)

    @pl.when(step == 0)
    def _():
        acc[...] = jnp.zeros_like(acc)
        for src in range(sources):
            for grp in range(groups):
                for row in range(rows):
                    start = (row * groups + grp) * rank_rows
                    lhs[start : start + rank_rows, src * points : (src + 1) * points] = x_ref[
                        src, grp, row
                    ]

    span = groups * rank_rows
    block_rows = min(rows, 2) * span
    for start in range(0, rows * span, block_rows):
        values = lhs[start : start + block_rows, :]
        spectra = jnp.dot(values, high_ref[...], preferred_element_type=jnp.float32)
        spectra += jnp.dot(values, low_ref[...], preferred_element_type=jnp.float32)
        for part in range(0, block_rows, span):
            row = (start + part) // span
            scaled = spectra[part : part + span] * weight_ref[0, row]
            top = scaled.astype(jnp.bfloat16)
            rest = (scaled - top.astype(jnp.float32)).astype(jnp.bfloat16)
            xh_ref[row] = top
            xl_ref[row] = rest
            acc[...] += lax.dot_general(
                jnp.concatenate([top, rest], axis=0), top, NT_DIMS, preferred_element_type=jnp.float32
            )

    @pl.when(step == pl.num_programs(0) - 1)
    def _():
        cross = acc[span:, :]
        gram_ref[...] = acc[:span, :] + (cross + cross.T)


def spectra_and_gram(blocks, row_weight, table_high, table_low):
    sources, groups, rows, rank_rows, points = blocks.shape
    lons, cols = table_high.shape
    span = groups * rank_rows
    modes = jax.ShapeDtypeStruct((rows, span, cols), jnp.bfloat16)
    return pl.pallas_call(
        spectra_kernel,
        grid=(cols // COL_TILE,),
        in_specs=[
            pl.BlockSpec(memory_space=pltpu.SMEM),
            pl.BlockSpec(blocks.shape, lambda i: (0, 0, 0, 0, 0)),
            pl.BlockSpec((lons, COL_TILE), lambda i: (0, i)),
            pl.BlockSpec((lons, COL_TILE), lambda i: (0, i)),
        ],
        out_specs=[
            pl.BlockSpec((rows, span, COL_TILE), lambda i: (0, 0, i)),
            pl.BlockSpec((rows, span, COL_TILE), lambda i: (0, 0, i)),
            pl.BlockSpec((span, span), lambda i: (0, 0)),
        ],
        out_shape=[modes, modes, jax.ShapeDtypeStruct((span, span), jnp.float32)],
        scratch_shapes=[
            pltpu.VMEM((rows * span, lons), jnp.bfloat16),
            pltpu.VMEM((2 * span, span), jnp.float32),
        ],
        compiler_params=pltpu.CompilerParams(vmem_limit_bytes=48 * 2**20),
        cost_estimate=pl.CostEstimate(
            flops=4 * rows * span * lons * cols,
            bytes_accessed=2 * blocks.size + 4 * lons * cols + 4 * rows * span * cols,
            transcendentals=0,
        ),
    )(row_weight.reshape(1, rows), blocks, table_high, table_low)


def dot_full(first, second, dims=(((1,), (0,)), ((), ()))):
    return lax.dot_general(
        first, second, dims, precision=highest, preferred_element_type=jnp.float32
    )


def eliminate(work, size):
    height, width = work.shape
    row_ids = lax.broadcasted_iota(jnp.int32, (height, width), 0)
    result = jnp.zeros_like(work)
    for col in range(size):
        pivot = work[col : col + 1, :]
        inverse = lax.rsqrt(work[col : col + 1, col : col + 1])
        scaled_row = pivot * inverse
        factor = work[:, col : col + 1] * inverse
        result = jnp.where(row_ids == col, scaled_row, result)
        work = work - factor * scaled_row
    return result


def merge_kernel(gram_ref, test_ref, xh_ref, xl_ref, out_ref, mix_ref):
    rank = test_ref.shape[1]
    row = pl.program_id(0)

    @pl.when(row == 0)
    def _():
        gram = gram_ref[...]
        test = test_ref[...]
        sketch = dot_full(gram, test)
        sketch_t = dot_full(test, gram, (((0,), (0,)), ((), ())))
        sketch_gram = dot_full(sketch_t, gram)
        power = dot_full(sketch_gram, sketch)
        power = 0.5 * (power + power.T)
        solved = eliminate(jnp.concatenate([power, jnp.zeros_like(power), sketch_gram, sketch_t], axis=1), rank)
        projected = solved[:, 2 * rank : 4 * rank]
        unmixed = solved[:, 4 * rank : 6 * rank]
        inner = dot_full(projected, projected, NT_DIMS)
        upper = eliminate(0.5 * (inner + inner.T), rank)
        col_ids = lax.broadcasted_iota(jnp.int32, upper.shape, 1)
        row_ids = lax.broadcasted_iota(jnp.int32, upper.shape, 0)
        mixing = dot_full(jnp.where(col_ids >= row_ids, upper, 0.0), unmixed)
        top = mixing.astype(jnp.bfloat16)
        rest = (mixing - top.astype(jnp.float32)).astype(jnp.bfloat16)
        mix_ref[:rank, : 2 * rank] = top
        mix_ref[:rank, 2 * rank :] = top
        mix_ref[rank:, : 2 * rank] = rest
        mix_ref[rank:, 2 * rank :] = jnp.zeros_like(rest)

    stacked = jnp.concatenate([xh_ref[0], xl_ref[0]], axis=0)
    both = jnp.dot(mix_ref[...], stacked, preferred_element_type=jnp.float32)
    out_ref[...] = both[:rank] + both[rank:]


def merge_and_mix(gram, test_matrix, modes_high, modes_low):
    rows, span, cols = modes_high.shape
    rank = test_matrix.shape[1]
    return pl.pallas_call(
        merge_kernel,
        grid=(rows,),
        in_specs=[
            pl.BlockSpec(gram.shape, lambda i: (0, 0)),
            pl.BlockSpec(test_matrix.shape, lambda i: (0, 0)),
            pl.BlockSpec((1, span, cols), lambda i: (i, 0, 0)),
            pl.BlockSpec((1, span, cols), lambda i: (i, 0, 0)),
        ],
        out_specs=pl.BlockSpec((rank, cols), lambda i: (0, i)),
        out_shape=jax.ShapeDtypeStruct((rank, rows * cols), jnp.float32),
        scratch_shapes=[pltpu.VMEM((2 * rank, 2 * span), jnp.bfloat16)],
        compiler_params=pltpu.CompilerParams(vmem_limit_bytes=32 * 2**20),
    )(gram, test_matrix, modes_high, modes_low)


def summed(array, axes):
    for axis in axes:
        for distance in range(lax.axis_size(axis).bit_length() - 1):
            array = array + swapped(array, axis, distance)
    return array


def local_pair(snapshots, test_matrix):
    points, rank_rows, total_rows = snapshots.shape
    lon_count, group_count = lax.axis_size("lon"), lax.axis_size("tm")
    dev_rows = total_rows // (lon_count * group_count)
    first_row = (lax.axis_index("lon") * group_count + lax.axis_index("tm")) * dev_rows
    row_weight = area_weight(first_row, dev_rows, NTH)
    table_high, table_low = split_table(NPH, MMAX)
    blocks = lax.all_to_all(
        snapshots.transpose(2, 1, 0), ("lon", "tm"), split_axis=0, concat_axis=0, tiled=True
    ).reshape(lon_count, group_count, dev_rows, rank_rows, points)
    modes_high, modes_low, gram = spectra_and_gram(blocks, row_weight, table_high, table_low)
    gram = summed(gram, ("lon", "tm"))
    return merge_and_mix(gram, test_matrix, modes_high, modes_low)


def solution(mesh):
    lon_count, group_count = mesh.shape["lon"], mesh.shape["tm"]
    whole_rows = NTH % (lon_count * group_count) == 0
    return jax.shard_map(
        local_pair if group_count == 2 and whole_rows else local_tree,
        mesh=mesh,
        in_specs=(P("lon", "tm", None), P()),
        out_specs=P(None, ("lon", "tm")),
        check_vma=False,
    )
```

```python
import functools
import math

import jax
import jax.numpy as jnp
from jax import lax
from jax.experimental import pallas as pl
from jax.experimental.pallas import tpu as pltpu
from jax.sharding import PartitionSpec as P

NPH = 2048
MMAX = 640
NTH = 256
COL_TILE = 256
LANES = 128
PIVOTS = 4
VMEM_BYTES = 59 * 2**20


highest = lax.Precision.HIGHEST
NT_DIMS = (((1,), (1,)), ((), ()))


def swapped(array, axis, distance):
    return lax.ppermute(array, axis, [(i, i ^ 1 << distance) for i in range(lax.axis_size(axis))])


def matmul(first_op, second_op):
    return jnp.dot(first_op, second_op, precision=highest, preferred_element_type=jnp.float32)


def spectral_table(points, wave_count):
    lon_ids = jnp.arange(points, dtype=jnp.int32)
    col_ids = jnp.arange(2 * wave_count, dtype=jnp.int32)
    wavenumber = jnp.where(col_ids < wave_count, col_ids, col_ids - wave_count + 1)
    phase_index = lon_ids[:, None] * wavenumber[None, :] % points
    angles = 2.0 * math.pi / points * phase_index.astype(jnp.float32)
    trig_value = jnp.where(col_ids[None, :] < wave_count, jnp.cos(angles), jnp.sin(angles))
    col_scale = math.sqrt(2.0 / points) / jnp.sqrt(
        1.0 + 4.0 * wavenumber.astype(jnp.float32) / wave_count
    )
    return trig_value * col_scale[None, :]


def area_weight(start_row, row_count, total_rows):
    row_ids = start_row + jnp.arange(row_count, dtype=jnp.int32)
    colatitude = math.pi * (row_ids.astype(jnp.float32) + 0.5) / (2.0 * total_rows)
    return jnp.sqrt(jnp.sin(colatitude))


def merge_gram(gram_matrix, test_matrix):
    sketch = matmul(gram_matrix, test_matrix)
    sketch_gram = matmul(sketch.T, gram_matrix)
    power_gram = matmul(sketch_gram, sketch)
    power_gram = 0.5 * (power_gram + power_gram.T)
    chol_first = jnp.linalg.cholesky(power_gram)
    projected = lax.linalg.triangular_solve(chol_first, sketch_gram, left_side=True, lower=True)
    proj_gram = matmul(projected, projected.T)
    chol_second = jnp.linalg.cholesky(0.5 * (proj_gram + proj_gram.T))
    unmixed = lax.linalg.triangular_solve(chol_first, sketch.T, left_side=True, lower=True)
    mixing = matmul(chol_second.T, unmixed)
    return (mixing, matmul(chol_second.T, chol_second))


def block_gram(low_energy, cross_term, high_energy):
    top_rows = jnp.concatenate([low_energy, cross_term], axis=1)
    bottom_rows = jnp.concatenate([cross_term.T, high_energy], axis=1)
    return jnp.concatenate([top_rows, bottom_rows], axis=0)


def combine_pair(mixing, low_modes, high_modes):
    rank_rows = low_modes.shape[0]
    return matmul(mixing[:, :rank_rows], low_modes) + matmul(mixing[:, rank_rows:], high_modes)


def own_columns(modes_flat, group_index, group_count):
    col_count = modes_flat.shape[1] // group_count
    return lax.dynamic_slice_in_dim(modes_flat, group_index * col_count, col_count, 1)


def local_tree(snapshots, test_matrix):
    dev_rows = NTH // lax.axis_size("lon")
    dft_table = spectral_table(NPH, MMAX)
    row_weight = area_weight(lax.axis_index("lon") * dev_rows, dev_rows, NTH)
    spectra = jnp.einsum(
        "pst,pk->stk",
        lax.all_to_all(snapshots, "lon", split_axis=2, concat_axis=0, tiled=True).astype(
            jnp.float32
        ),
        dft_table,
        precision=highest,
    )
    spectra = spectra * row_weight[None, :, None]
    rank_rows = spectra.shape[0]
    modes_now = spectra.reshape(rank_rows, -1)
    levels_count = lax.axis_size("tm").bit_length() - 1
    group_index = lax.axis_index("tm")
    group_count = lax.axis_size("tm")
    energy = lax.psum(matmul(modes_now, modes_now.T), "lon")
    start_level = 0
    for tree_level in range(start_level, levels_count):
        partner_modes, partner_energy = swapped((modes_now, energy), "tm", tree_level)
        is_upper = group_index // 2**tree_level % 2 == 1
        low_modes = jnp.where(is_upper, partner_modes, modes_now)
        high_modes = jnp.where(is_upper, modes_now, partner_modes)
        low_energy = jnp.where(is_upper, partner_energy, energy)
        high_energy = jnp.where(is_upper, energy, partner_energy)
        cross_term = lax.psum(matmul(low_modes, high_modes.T), "lon")
        mixing, energy = merge_gram(block_gram(low_energy, cross_term, high_energy), test_matrix)
        modes_now = combine_pair(mixing, low_modes, high_modes)
    return own_columns(modes_now, group_index, group_count)


def split_table(points, wave_count):
    table = spectral_table(points, wave_count)
    high = lax.reduce_precision(table, 8, 7)
    return high.astype(jnp.bfloat16), (table - high).astype(jnp.bfloat16)


def spectra_kernel(weight_ref, x_ref, high_ref, low_ref, xh_ref, xl_ref, gram_ref, lhs, acc):
    sources, groups, rows, rank_rows, points = x_ref.shape
    step = pl.program_id(0)

    @pl.when(step == 0)
    def _():
        acc[...] = jnp.zeros_like(acc)
        for src in range(sources):
            for grp in range(groups):
                for row in range(rows):
                    start = (row * groups + grp) * rank_rows
                    lhs[start : start + rank_rows, src * points : (src + 1) * points] = x_ref[
                        src, grp, row
                    ]

    span = groups * rank_rows
    values = lhs[...]
    spectra = jnp.dot(values, high_ref[...], preferred_element_type=jnp.float32)
    spectra += jnp.dot(values, low_ref[...], preferred_element_type=jnp.float32)
    tops, rests = [], []
    for row in range(rows):
        scaled = spectra[row * span : (row + 1) * span] * weight_ref[0, row]
        top = scaled.astype(jnp.bfloat16)
        rest = (scaled - top.astype(jnp.float32)).astype(jnp.bfloat16)
        xh_ref[row] = top
        xl_ref[row] = rest
        tops.append(top)
        rests.append(rest)
    top = jnp.concatenate(tops, axis=1)
    both = jnp.concatenate([top, jnp.concatenate(rests, axis=1)], axis=0)
    acc[...] += lax.dot_general(both, top, NT_DIMS, preferred_element_type=jnp.float32)

    @pl.when(step == pl.num_programs(0) - 1)
    def _():
        cross = acc[span:, :]
        gram = acc[:span, :] + (cross + cross.T)
        gram_ref[:rank_rows, :] = gram[:rank_rows, :]
        low = gram[rank_rows:, rank_rows:]
        gram_ref[rank_rows:, :] = jnp.concatenate([low[: rank_rows // 2], low[rank_rows // 2 :]], axis=1)


def spectra_and_gram(blocks, row_weight, table_high, table_low):
    sources, groups, rows, rank_rows, points = blocks.shape
    lons, cols = table_high.shape
    span = groups * rank_rows
    packed = rank_rows + rank_rows // 2
    modes = jax.ShapeDtypeStruct((rows, span, cols), jnp.bfloat16)
    return pl.pallas_call(
        spectra_kernel,
        grid=(cols // COL_TILE,),
        in_specs=[
            pl.BlockSpec(memory_space=pltpu.SMEM),
            pl.BlockSpec(blocks.shape, lambda i: (0, 0, 0, 0, 0)),
            pl.BlockSpec((lons, COL_TILE), lambda i: (0, i)),
            pl.BlockSpec((lons, COL_TILE), lambda i: (0, i)),
        ],
        out_specs=[
            pl.BlockSpec((rows, span, COL_TILE), lambda i: (0, 0, i)),
            pl.BlockSpec((rows, span, COL_TILE), lambda i: (0, 0, i)),
            pl.BlockSpec((packed, span), lambda i: (0, 0)),
        ],
        out_shape=[modes, modes, jax.ShapeDtypeStruct((packed, span), jnp.float32)],
        scratch_shapes=[
            pltpu.VMEM((rows * span, lons), jnp.bfloat16),
            pltpu.VMEM((2 * span, span), jnp.float32),
        ],
        compiler_params=pltpu.CompilerParams(vmem_limit_bytes=VMEM_BYTES),
        cost_estimate=pl.CostEstimate(
            flops=4 * rows * span * lons * cols,
            bytes_accessed=2 * blocks.size + 4 * lons * cols + 4 * rows * span * cols,
            transcendentals=0,
        ),
    )(row_weight.reshape(1, rows), blocks, table_high, table_low)


def dot_full(first, second, dims=(((1,), (0,)), ((), ()))):
    return lax.dot_general(
        first, second, dims, precision=highest, preferred_element_type=jnp.float32
    )


def eliminate(work, size, out_ref):
    height, width = work.shape
    for col in range(0, size, PIVOTS):
        base = col // 8 * 8
        lead = col - base
        rows = [work[lead + i : lead + i + 1, :] for i in range(PIVOTS)]
        cols = [
            jnp.broadcast_to(work[:, col + i : col + i + 1], (height - base, LANES)) for i in range(PIVOTS)
        ]
        update = None
        for i in range(PIVOTS):
            inverse = lax.rsqrt(cols[i][lead + i : lead + i + 1, :])
            wide = jnp.concatenate([inverse] * (width // LANES), axis=1)
            solved = rows[i] * wide
            out_ref[col + i : col + i + 1, :] = solved
            factor = cols[i] * inverse
            for k in range(i + 1, PIVOTS):
                share = factor[lead + k : lead + k + 1, :]
                cols[k] = cols[k] - factor * share
                rows[k] = rows[k] - solved * jnp.concatenate([share] * (width // LANES), axis=1)
            term = jnp.concatenate([factor] * (width // LANES), axis=1) * solved
            update = term if update is None else update + term
        following = (col + PIVOTS) // 8 * 8 - base
        work = work[following:] - update[following:]


def add_up(parts):
    while len(parts) > 1:
        parts = [parts[i] + parts[i + 1] for i in range(0, len(parts), 2)]
    return parts[0]


def unpacked(packed):
    span = packed.shape[1]
    rank = span // 2
    low = jnp.concatenate([packed[rank:, :rank], packed[rank:, rank:]], axis=0)
    square = jnp.concatenate(
        [packed[:rank], jnp.concatenate([jnp.zeros_like(low), low], axis=1)], axis=0
    )
    row_ids = lax.broadcasted_iota(jnp.int32, square.shape, 0)
    col_ids = lax.broadcasted_iota(jnp.int32, square.shape, 1)
    return jnp.where((row_ids >= rank) & (col_ids < rank), square.T, square)


def merge_kernel(*refs):
    *part_refs, test_ref, xh_ref, xl_ref, out_ref, mix_ref, first_ref, second_ref = refs
    rank = test_ref.shape[1]
    row = pl.program_id(0)

    @pl.when(row == 0)
    def _():
        gram = unpacked(add_up([part[...] for part in part_refs]))
        test = test_ref[...]
        sketch = dot_full(gram, test)
        sketch_t = dot_full(test, gram, (((0,), (0,)), ((), ())))
        sketch_gram = dot_full(sketch_t, gram)
        power = dot_full(sketch_gram, sketch)
        power = 0.5 * (power + power.T)
        pad = jnp.zeros_like(power)
        eliminate(jnp.concatenate([power, pad, sketch_gram, sketch_t], axis=1), rank, first_ref)
        projected = first_ref[:, 2 * rank : 4 * rank]
        unmixed = first_ref[:, 4 * rank : 6 * rank]
        inner = dot_full(projected, projected, NT_DIMS)
        inner = 0.5 * (inner + inner.T)
        eliminate(jnp.concatenate([inner, pad], axis=1), rank, second_ref)
        upper = second_ref[:, :rank]
        col_ids = lax.broadcasted_iota(jnp.int32, upper.shape, 1)
        row_ids = lax.broadcasted_iota(jnp.int32, upper.shape, 0)
        mixing = dot_full(jnp.where(col_ids >= row_ids, upper, 0.0), unmixed)
        top = mixing.astype(jnp.bfloat16)
        rest = (mixing - top.astype(jnp.float32)).astype(jnp.bfloat16)
        mix_ref[:rank, : 2 * rank] = top
        mix_ref[:rank, 2 * rank :] = top
        mix_ref[rank:, : 2 * rank] = rest
        mix_ref[rank:, 2 * rank :] = jnp.zeros_like(rest)

    stacked = jnp.concatenate([xh_ref[0], xl_ref[0]], axis=0)
    both = jnp.dot(mix_ref[...], stacked, preferred_element_type=jnp.float32)
    out_ref[...] = both[:rank] + both[rank:]


def merge_and_mix(gram_parts, test_matrix, modes_high, modes_low):
    rows, span, cols = modes_high.shape
    rank = test_matrix.shape[1]
    return pl.pallas_call(
        merge_kernel,
        grid=(rows,),
        in_specs=[
            *[pl.BlockSpec(part.shape, lambda i: (0, 0)) for part in gram_parts],
            pl.BlockSpec(test_matrix.shape, lambda i: (0, 0)),
            pl.BlockSpec((1, span, cols), lambda i: (i, 0, 0)),
            pl.BlockSpec((1, span, cols), lambda i: (i, 0, 0)),
        ],
        out_specs=pl.BlockSpec((rank, cols), lambda i: (0, i)),
        out_shape=jax.ShapeDtypeStruct((rank, rows * cols), jnp.float32),
        scratch_shapes=[
            pltpu.VMEM((2 * rank, 2 * span), jnp.bfloat16),
            pltpu.VMEM((rank, 6 * rank), jnp.float32),
            pltpu.VMEM((rank, 2 * rank), jnp.float32),
        ],
        compiler_params=pltpu.CompilerParams(vmem_limit_bytes=VMEM_BYTES),
    )(*gram_parts, test_matrix, modes_high, modes_low)


def exchanged(array, axes, bits):
    count = lax.axis_size(axes)
    masks = [0]
    for bit in bits:
        masks += [mask | bit for mask in masks]
    return [array] + [
        lax.ppermute(array, axes, [(i, i ^ mask) for i in range(count)]) for mask in masks[1:]
    ]


def sum_parts(array, axes):
    bits = [1 << k for k in range(lax.axis_size(axes).bit_length() - 1)]
    parts = exchanged(array, axes, bits[:1])
    for group in (bits[1:2] + bits[-1:], *[bits[k : k + 2] for k in range(2, len(bits) - 1, 2)]):
        parts = exchanged(add_up(parts), axes, group)
    return parts


def local_pair(snapshots, test_matrix):
    points, rank_rows, total_rows = snapshots.shape
    lon_count, group_count = lax.axis_size("lon"), lax.axis_size("tm")
    dev_rows = total_rows // (lon_count * group_count)
    first_row = (lax.axis_index("lon") * group_count + lax.axis_index("tm")) * dev_rows
    row_weight = area_weight(first_row, dev_rows, NTH)
    table_high, table_low = split_table(NPH, MMAX)
    blocks = lax.all_to_all(
        snapshots.transpose(2, 1, 0), ("lon", "tm"), split_axis=0, concat_axis=0, tiled=True
    ).reshape(lon_count, group_count, dev_rows, rank_rows, points)
    modes_high, modes_low, gram = spectra_and_gram(blocks, row_weight, table_high, table_low)
    gram_parts = sum_parts(gram, ("tm", "lon"))
    return merge_and_mix(gram_parts, test_matrix, modes_high, modes_low)


def solution(mesh):
    lon_count, group_count = mesh.shape["lon"], mesh.shape["tm"]
    device_count = lon_count * group_count
    whole_rows = NTH % device_count == 0 and device_count & (device_count - 1) == 0
    return jax.shard_map(
        local_pair if group_count == 2 and whole_rows else local_tree,
        mesh=mesh,
        in_specs=(P("lon", "tm", None), P()),
        out_specs=P(None, ("lon", "tm")),
        check_vma=False,
    )
```

```python
import functools
import math

import jax
import jax.numpy as jnp
from jax import lax
from jax.experimental import pallas as pl
from jax.experimental.pallas import tpu as pltpu
from jax.sharding import PartitionSpec as P

NPH = 2048
MMAX = 640
NTH = 256
COL_TILE = 256
LANES = 128
PIVOTS = 4
SNAPSHOT_TILE = 16
EARLY_ROWS = 6
VMEM_BYTES = 51 * 2**20


highest = lax.Precision.HIGHEST
NT_DIMS = (((1,), (1,)), ((), ()))


def swapped(array, axis, distance):
    return lax.ppermute(array, axis, [(i, i ^ 1 << distance) for i in range(lax.axis_size(axis))])


def matmul(first_op, second_op):
    return jnp.dot(first_op, second_op, precision=highest, preferred_element_type=jnp.float32)


def spectral_table(points, wave_count):
    lon_ids = jnp.arange(points, dtype=jnp.int32)
    col_ids = jnp.arange(2 * wave_count, dtype=jnp.int32)
    wavenumber = jnp.where(col_ids < wave_count, col_ids, col_ids - wave_count + 1)
    phase_index = lon_ids[:, None] * wavenumber[None, :] % points
    angles = 2.0 * math.pi / points * phase_index.astype(jnp.float32)
    trig_value = jnp.where(col_ids[None, :] < wave_count, jnp.cos(angles), jnp.sin(angles))
    col_scale = math.sqrt(2.0 / points) / jnp.sqrt(
        1.0 + 4.0 * wavenumber.astype(jnp.float32) / wave_count
    )
    return trig_value * col_scale[None, :]


def area_weight(start_row, row_count, total_rows):
    row_ids = start_row + jnp.arange(row_count, dtype=jnp.int32)
    colatitude = math.pi * (row_ids.astype(jnp.float32) + 0.5) / (2.0 * total_rows)
    return jnp.sqrt(jnp.sin(colatitude))


def merge_gram(gram_matrix, test_matrix):
    sketch = matmul(gram_matrix, test_matrix)
    sketch_gram = matmul(sketch.T, gram_matrix)
    power_gram = matmul(sketch_gram, sketch)
    power_gram = 0.5 * (power_gram + power_gram.T)
    chol_first = jnp.linalg.cholesky(power_gram)
    projected = lax.linalg.triangular_solve(chol_first, sketch_gram, left_side=True, lower=True)
    proj_gram = matmul(projected, projected.T)
    chol_second = jnp.linalg.cholesky(0.5 * (proj_gram + proj_gram.T))
    unmixed = lax.linalg.triangular_solve(chol_first, sketch.T, left_side=True, lower=True)
    mixing = matmul(chol_second.T, unmixed)
    return (mixing, matmul(chol_second.T, chol_second))


def block_gram(low_energy, cross_term, high_energy):
    top_rows = jnp.concatenate([low_energy, cross_term], axis=1)
    bottom_rows = jnp.concatenate([cross_term.T, high_energy], axis=1)
    return jnp.concatenate([top_rows, bottom_rows], axis=0)


def combine_pair(mixing, low_modes, high_modes):
    rank_rows = low_modes.shape[0]
    return matmul(mixing[:, :rank_rows], low_modes) + matmul(mixing[:, rank_rows:], high_modes)


def own_columns(modes_flat, group_index, group_count):
    col_count = modes_flat.shape[1] // group_count
    return lax.dynamic_slice_in_dim(modes_flat, group_index * col_count, col_count, 1)


def local_tree(snapshots, test_matrix):
    dev_rows = NTH // lax.axis_size("lon")
    dft_table = spectral_table(NPH, MMAX)
    row_weight = area_weight(lax.axis_index("lon") * dev_rows, dev_rows, NTH)
    spectra = jnp.einsum(
        "pst,pk->stk",
        lax.all_to_all(snapshots, "lon", split_axis=2, concat_axis=0, tiled=True).astype(
            jnp.float32
        ),
        dft_table,
        precision=highest,
    )
    spectra = spectra * row_weight[None, :, None]
    rank_rows = spectra.shape[0]
    modes_now = spectra.reshape(rank_rows, -1)
    levels_count = lax.axis_size("tm").bit_length() - 1
    group_index = lax.axis_index("tm")
    group_count = lax.axis_size("tm")
    energy = lax.psum(matmul(modes_now, modes_now.T), "lon")
    start_level = 0
    for tree_level in range(start_level, levels_count):
        partner_modes, partner_energy = swapped((modes_now, energy), "tm", tree_level)
        is_upper = group_index // 2**tree_level % 2 == 1
        low_modes = jnp.where(is_upper, partner_modes, modes_now)
        high_modes = jnp.where(is_upper, modes_now, partner_modes)
        low_energy = jnp.where(is_upper, partner_energy, energy)
        high_energy = jnp.where(is_upper, energy, partner_energy)
        cross_term = lax.psum(matmul(low_modes, high_modes.T), "lon")
        mixing, energy = merge_gram(block_gram(low_energy, cross_term, high_energy), test_matrix)
        modes_now = combine_pair(mixing, low_modes, high_modes)
    return own_columns(modes_now, group_index, group_count)


def split_table(points, wave_count):
    table = spectral_table(points, wave_count)
    high = lax.reduce_precision(table, 8, 7)
    return jnp.stack([high.astype(jnp.bfloat16), (table - high).astype(jnp.bfloat16)])


def relayout_kernel(x_ref, first_ref, last_ref):
    points, some, total = x_ref.shape
    devices, split = first_ref.shape[:2]
    by_snapshot = jnp.transpose(x_ref[...], (1, 0, 2))
    turned = jnp.stack([by_snapshot[i].T for i in range(some)], axis=0)
    rows = jnp.transpose(turned, (1, 0, 2)).reshape(devices, total // devices, some, points)
    first_ref[...] = rows[:, :split]
    last_ref[...] = rows[:, split:]


def relayout(snapshots, devices, split):
    points, rank_rows, total = snapshots.shape
    some = SNAPSHOT_TILE
    cuts = (split, total // devices - split)
    return pl.pallas_call(
        relayout_kernel,
        grid=(rank_rows // some,),
        in_specs=[pl.BlockSpec((points, some, total), lambda i: (0, i, 0))],
        out_specs=[pl.BlockSpec((devices, cut, some, points), lambda i: (0, 0, i, 0)) for cut in cuts],
        out_shape=[
            jax.ShapeDtypeStruct((devices, cut, rank_rows, points), snapshots.dtype) for cut in cuts
        ],
        compiler_params=pltpu.CompilerParams(vmem_limit_bytes=VMEM_BYTES),
    )(snapshots)


def spectra_kernel(*refs, first_row):
    weight_ref, x_ref, table_ref, *before, modes_ref, gram_ref, lhs, acc = refs
    sources, groups, rows, rank_rows, points = x_ref.shape
    step = pl.program_id(0)

    @pl.when(step == 0)
    def _():
        acc[...] = jnp.zeros_like(acc)
        for src in range(sources):
            for grp in range(groups):
                for row in range(rows):
                    start = (row * groups + grp) * rank_rows
                    lhs[start : start + rank_rows, src * points : (src + 1) * points] = x_ref[
                        src, grp, row
                    ]

    span = groups * rank_rows
    values = lhs[...]
    spectra = jnp.dot(values, table_ref[0], preferred_element_type=jnp.float32)
    spectra += jnp.dot(values, table_ref[1], preferred_element_type=jnp.float32)
    tops, rests = [], []
    for row in range(rows):
        scaled = spectra[row * span : (row + 1) * span] * weight_ref[0, first_row + row]
        top = scaled.astype(jnp.bfloat16)
        rest = (scaled - top.astype(jnp.float32)).astype(jnp.bfloat16)
        modes_ref[row, :span] = top
        modes_ref[row, span:] = rest
        tops.append(top)
        rests.append(rest)
    top = jnp.concatenate(tops, axis=1)
    both = jnp.concatenate([top, jnp.concatenate(rests, axis=1)], axis=0)
    acc[...] += lax.dot_general(both, top, NT_DIMS, preferred_element_type=jnp.float32)

    @pl.when(step == pl.num_programs(0) - 1)
    def _():
        cross = acc[span:, :]
        gram = acc[:span, :] + (cross + cross.T)
        low = gram[rank_rows:, rank_rows:]
        low = jnp.concatenate([low[: rank_rows // 2], low[rank_rows // 2 :]], axis=1)
        packed = jnp.concatenate([gram[:rank_rows], low], axis=0)
        for ref in before:
            packed += ref[...]
        gram_ref[...] = packed


def spectra_and_gram(blocks, row_weight, table, first_row, *before):
    sources, groups, rows, rank_rows, points = blocks.shape
    _, lons, cols = table.shape
    span = groups * rank_rows
    packed = (rank_rows + rank_rows // 2, span)
    return pl.pallas_call(
        functools.partial(spectra_kernel, first_row=first_row),
        grid=(cols // COL_TILE,),
        in_specs=[
            pl.BlockSpec(memory_space=pltpu.SMEM),
            pl.BlockSpec(blocks.shape, lambda i: (0, 0, 0, 0, 0)),
            pl.BlockSpec((2, lons, COL_TILE), lambda i: (0, 0, i)),
            *[pl.BlockSpec(packed, lambda i: (0, 0)) for _ in before],
        ],
        out_specs=[
            pl.BlockSpec((rows, 2 * span, COL_TILE), lambda i: (0, 0, i)),
            pl.BlockSpec(packed, lambda i: (0, 0)),
        ],
        out_shape=[
            jax.ShapeDtypeStruct((rows, 2 * span, cols), jnp.bfloat16),
            jax.ShapeDtypeStruct(packed, jnp.float32),
        ],
        scratch_shapes=[
            pltpu.VMEM((rows * span, lons), jnp.bfloat16),
            pltpu.VMEM((2 * span, span), jnp.float32),
        ],
        compiler_params=pltpu.CompilerParams(vmem_limit_bytes=VMEM_BYTES),
        cost_estimate=pl.CostEstimate(
            flops=4 * rows * span * lons * cols,
            bytes_accessed=2 * blocks.size + 4 * lons * cols + 4 * rows * span * cols,
            transcendentals=0,
        ),
    )(row_weight.reshape(1, -1), blocks, table, *before)


def dot_full(first, second, dims=(((1,), (0,)), ((), ()))):
    return lax.dot_general(
        first, second, dims, precision=highest, preferred_element_type=jnp.float32
    )


def eliminate(work, size, out_ref):
    height, width = work.shape
    for col in range(0, size, PIVOTS):
        base = col // 8 * 8
        lead = col - base
        rows = [work[lead + i : lead + i + 1, :] for i in range(PIVOTS)]
        cols = [
            jnp.broadcast_to(work[:, col + i : col + i + 1], (height - base, LANES)) for i in range(PIVOTS)
        ]
        update = None
        for i in range(PIVOTS):
            inverse = lax.rsqrt(cols[i][lead + i : lead + i + 1, :])
            wide = jnp.concatenate([inverse] * (width // LANES), axis=1)
            solved = rows[i] * wide
            out_ref[col + i : col + i + 1, :] = solved
            factor = cols[i] * inverse
            for k in range(i + 1, PIVOTS):
                share = factor[lead + k : lead + k + 1, :]
                cols[k] = cols[k] - factor * share
                rows[k] = rows[k] - solved * jnp.concatenate([share] * (width // LANES), axis=1)
            term = jnp.concatenate([factor] * (width // LANES), axis=1) * solved
            update = term if update is None else update + term
        following = (col + PIVOTS) // 8 * 8 - base
        work = work[following:] - update[following:]


def add_up(parts):
    while len(parts) > 1:
        parts = [parts[i] + parts[i + 1] for i in range(0, len(parts), 2)]
    return parts[0]


def unpacked(packed):
    span = packed.shape[1]
    rank = span // 2
    low = jnp.concatenate([packed[rank:, :rank], packed[rank:, rank:]], axis=0)
    square = jnp.concatenate(
        [packed[:rank], jnp.concatenate([jnp.zeros_like(low), low], axis=1)], axis=0
    )
    row_ids = lax.broadcasted_iota(jnp.int32, square.shape, 0)
    col_ids = lax.broadcasted_iota(jnp.int32, square.shape, 1)
    return jnp.where((row_ids >= rank) & (col_ids < rank), square.T, square)


def merge_kernel(*refs, split):
    *part_refs, test_ref, early_ref, late_ref, out_ref, mix_ref, first_ref, second_ref = refs
    rank = test_ref.shape[0]
    row = pl.program_id(0)

    @pl.when(row == 0)
    def _():
        gram = unpacked(add_up([part[...] for part in part_refs]))
        test_t = test_ref[...]
        sketch = dot_full(gram, test_t, NT_DIMS)
        sketch_t = dot_full(test_t, gram)
        sketch_gram = dot_full(sketch_t, gram)
        power = dot_full(sketch_gram, sketch)
        power = 0.5 * (power + power.T)
        pad = jnp.zeros_like(power)
        eliminate(jnp.concatenate([power, pad, sketch_gram, sketch_t], axis=1), rank, first_ref)
        projected = first_ref[:, 2 * rank : 4 * rank]
        unmixed = first_ref[:, 4 * rank : 6 * rank]
        inner = dot_full(projected, projected, NT_DIMS)
        inner = 0.5 * (inner + inner.T)
        eliminate(jnp.concatenate([inner, pad], axis=1), rank, second_ref)
        upper = second_ref[:, :rank]
        col_ids = lax.broadcasted_iota(jnp.int32, upper.shape, 1)
        row_ids = lax.broadcasted_iota(jnp.int32, upper.shape, 0)
        mixing = dot_full(jnp.where(col_ids >= row_ids, upper, 0.0), unmixed)
        top = mixing.astype(jnp.bfloat16)
        rest = (mixing - top.astype(jnp.float32)).astype(jnp.bfloat16)
        mix_ref[:rank, : 2 * rank] = top
        mix_ref[:rank, 2 * rank :] = top
        mix_ref[rank:, : 2 * rank] = rest
        mix_ref[rank:, 2 * rank :] = jnp.zeros_like(rest)

    def mix(modes):
        both = jnp.dot(mix_ref[...], modes, preferred_element_type=jnp.float32)
        out_ref[...] = both[:rank] + both[rank:]

    @pl.when(row < split)
    def _():
        mix(early_ref[0])

    @pl.when(row >= split)
    def _():
        mix(late_ref[0])


def merge_and_mix(gram_parts, test_matrix, early, late):
    split, height, cols = early.shape
    rows = split + late.shape[0]
    rank = test_matrix.shape[1]
    return pl.pallas_call(
        functools.partial(merge_kernel, split=split),
        grid=(rows,),
        in_specs=[
            *[pl.BlockSpec(part.shape, lambda i: (0, 0)) for part in gram_parts],
            pl.BlockSpec((rank, 2 * rank), lambda i: (0, 0)),
            pl.BlockSpec((1, height, cols), lambda i: (jnp.minimum(i, split - 1), 0, 0)),
            pl.BlockSpec((1, height, cols), lambda i: (jnp.maximum(i - split, 0), 0, 0)),
        ],
        out_specs=pl.BlockSpec((rank, cols), lambda i: (0, i)),
        out_shape=jax.ShapeDtypeStruct((rank, rows * cols), jnp.float32),
        scratch_shapes=[
            pltpu.VMEM((2 * rank, height), jnp.bfloat16),
            pltpu.VMEM((rank, 6 * rank), jnp.float32),
            pltpu.VMEM((rank, 2 * rank), jnp.float32),
        ],
        compiler_params=pltpu.CompilerParams(vmem_limit_bytes=VMEM_BYTES),
    )(*gram_parts, test_matrix.T, early, late)


def exchanged(array, axes, bits):
    count = lax.axis_size(axes)
    masks = [0]
    for bit in bits:
        masks += [mask | bit for mask in masks]
    return [array] + [
        lax.ppermute(array, axes, [(i, i ^ mask) for i in range(count)]) for mask in masks[1:]
    ]


def sum_parts(array, axes):
    bits = [1 << k for k in range(lax.axis_size(axes).bit_length() - 1)]
    parts = exchanged(array, axes, bits[:1])
    for group in (bits[1:2] + bits[-1:], *[bits[k : k + 2] for k in range(2, len(bits) - 1, 2)]):
        parts = exchanged(add_up(parts), axes, group)
    return parts


def local_pair(snapshots, test_matrix):
    points, rank_rows, total_rows = snapshots.shape
    lon_count, group_count = lax.axis_size("lon"), lax.axis_size("tm")
    dev_rows = total_rows // (lon_count * group_count)
    first_row = (lax.axis_index("lon") * group_count + lax.axis_index("tm")) * dev_rows
    row_weight = area_weight(first_row, dev_rows, NTH)
    table = split_table(NPH, MMAX)
    split = EARLY_ROWS * dev_rows // 8
    early, late = relayout(snapshots, lon_count * group_count, split)
    late, table = lax.optimization_barrier((late, table))
    modes, gram = [], []
    for first, part in ((0, early), (split, late)):
        blocks = lax.all_to_all(part, ("lon", "tm"), split_axis=0, concat_axis=0, tiled=True)
        blocks = blocks.reshape(lon_count, group_count, -1, rank_rows, points)
        spectra, *gram = spectra_and_gram(blocks, row_weight, table, first, *gram)
        modes.append(spectra)
    return merge_and_mix(sum_parts(gram[0], ("tm", "lon")), test_matrix, *modes)


def solution(mesh):
    lon_count, group_count = mesh.shape["lon"], mesh.shape["tm"]
    device_count = lon_count * group_count
    whole_rows = NTH % device_count == 0 and device_count & (device_count - 1) == 0
    return jax.shard_map(
        local_pair if group_count == 2 and whole_rows else local_tree,
        mesh=mesh,
        in_specs=(P("lon", "tm", None), P()),
        out_specs=P(None, ("lon", "tm")),
        check_vma=False,
    )
```

```python
import functools
import math

import jax
import jax.numpy as jnp
from jax import lax
from jax.experimental import pallas as pl
from jax.experimental.pallas import tpu as pltpu
from jax.sharding import PartitionSpec as P

NPH = 2048
MMAX = 640
NTH = 256
COL_TILE = 256
LANES = 128
PIVOTS = 4
SNAPSHOT_TILE = 16
EARLY_ROWS = 6
VMEM_BYTES = 52 * 2**20
MERGE_VMEM_BYTES = 61000 * 2**10


highest = lax.Precision.HIGHEST
NT_DIMS = (((1,), (1,)), ((), ()))


def swapped(array, axis, distance):
    return lax.ppermute(array, axis, [(i, i ^ 1 << distance) for i in range(lax.axis_size(axis))])


def matmul(first_op, second_op):
    return jnp.dot(first_op, second_op, precision=highest, preferred_element_type=jnp.float32)


def spectral_table(points, wave_count, row_count):
    lon_ids = jnp.arange(row_count, dtype=jnp.int32)
    col_ids = jnp.arange(2 * wave_count, dtype=jnp.int32)
    wavenumber = jnp.where(col_ids < wave_count, col_ids, col_ids - wave_count + 1)
    phase_index = lon_ids[:, None] * wavenumber[None, :] % points
    angles = 2.0 * math.pi / points * phase_index.astype(jnp.float32)
    trig_value = jnp.where(col_ids[None, :] < wave_count, jnp.cos(angles), jnp.sin(angles))
    col_scale = math.sqrt(2.0 / points) / jnp.sqrt(
        1.0 + 4.0 * wavenumber.astype(jnp.float32) / wave_count
    )
    return trig_value * col_scale[None, :]


def area_weight(start_row, row_count, total_rows):
    row_ids = start_row + jnp.arange(row_count, dtype=jnp.int32)
    colatitude = math.pi * (row_ids.astype(jnp.float32) + 0.5) / (2.0 * total_rows)
    return jnp.sqrt(jnp.sin(colatitude))


def merge_gram(gram_matrix, test_matrix):
    sketch = matmul(gram_matrix, test_matrix)
    sketch_gram = matmul(sketch.T, gram_matrix)
    power_gram = matmul(sketch_gram, sketch)
    power_gram = 0.5 * (power_gram + power_gram.T)
    chol_first = jnp.linalg.cholesky(power_gram)
    projected = lax.linalg.triangular_solve(chol_first, sketch_gram, left_side=True, lower=True)
    proj_gram = matmul(projected, projected.T)
    chol_second = jnp.linalg.cholesky(0.5 * (proj_gram + proj_gram.T))
    unmixed = lax.linalg.triangular_solve(chol_first, sketch.T, left_side=True, lower=True)
    mixing = matmul(chol_second.T, unmixed)
    return (mixing, matmul(chol_second.T, chol_second))


def block_gram(low_energy, cross_term, high_energy):
    top_rows = jnp.concatenate([low_energy, cross_term], axis=1)
    bottom_rows = jnp.concatenate([cross_term.T, high_energy], axis=1)
    return jnp.concatenate([top_rows, bottom_rows], axis=0)


def combine_pair(mixing, low_modes, high_modes):
    rank_rows = low_modes.shape[0]
    return matmul(mixing[:, :rank_rows], low_modes) + matmul(mixing[:, rank_rows:], high_modes)


def own_columns(modes_flat, group_index, group_count):
    col_count = modes_flat.shape[1] // group_count
    return lax.dynamic_slice_in_dim(modes_flat, group_index * col_count, col_count, 1)


def local_tree(snapshots, test_matrix):
    dev_rows = NTH // lax.axis_size("lon")
    dft_table = spectral_table(NPH, MMAX, NPH)
    row_weight = area_weight(lax.axis_index("lon") * dev_rows, dev_rows, NTH)
    spectra = jnp.einsum(
        "pst,pk->stk",
        lax.all_to_all(snapshots, "lon", split_axis=2, concat_axis=0, tiled=True).astype(
            jnp.float32
        ),
        dft_table,
        precision=highest,
    )
    spectra = spectra * row_weight[None, :, None]
    rank_rows = spectra.shape[0]
    modes_now = spectra.reshape(rank_rows, -1)
    levels_count = lax.axis_size("tm").bit_length() - 1
    group_index = lax.axis_index("tm")
    group_count = lax.axis_size("tm")
    energy = lax.psum(matmul(modes_now, modes_now.T), "lon")
    start_level = 0
    for tree_level in range(start_level, levels_count):
        partner_modes, partner_energy = swapped((modes_now, energy), "tm", tree_level)
        is_upper = group_index // 2**tree_level % 2 == 1
        low_modes = jnp.where(is_upper, partner_modes, modes_now)
        high_modes = jnp.where(is_upper, modes_now, partner_modes)
        low_energy = jnp.where(is_upper, partner_energy, energy)
        high_energy = jnp.where(is_upper, energy, partner_energy)
        cross_term = lax.psum(matmul(low_modes, high_modes.T), "lon")
        mixing, energy = merge_gram(block_gram(low_energy, cross_term, high_energy), test_matrix)
        modes_now = combine_pair(mixing, low_modes, high_modes)
    return own_columns(modes_now, group_index, group_count)


def split_table(points, wave_count):
    table = spectral_table(points, wave_count, points // 2)
    high = lax.reduce_precision(table, 8, 7)
    return jnp.stack([high.astype(jnp.bfloat16), (table - high).astype(jnp.bfloat16)])


def relayout_kernel(x_ref, first_ref, last_ref):
    points, some, total = x_ref.shape
    devices, split = first_ref.shape[:2]
    by_snapshot = jnp.transpose(x_ref[...], (1, 0, 2))
    turned = jnp.stack([by_snapshot[i].T for i in range(some)], axis=0)
    rows = jnp.transpose(turned, (1, 0, 2)).reshape(devices, total // devices, some, points)
    first_ref[...] = rows[:, :split]
    last_ref[...] = rows[:, split:]


def relayout(snapshots, devices, split):
    points, rank_rows, total = snapshots.shape
    some = SNAPSHOT_TILE
    cuts = (split, total // devices - split)
    return pl.pallas_call(
        relayout_kernel,
        grid=(rank_rows // some,),
        in_specs=[pl.BlockSpec((points, some, total), lambda i: (0, i, 0))],
        out_specs=[pl.BlockSpec((devices, cut, some, points), lambda i: (0, 0, i, 0)) for cut in cuts],
        out_shape=[
            jax.ShapeDtypeStruct((devices, cut, rank_rows, points), snapshots.dtype) for cut in cuts
        ],
        compiler_params=pltpu.CompilerParams(vmem_limit_bytes=VMEM_BYTES),
    )(snapshots)


def spectra_kernel(*refs, first_row):
    weight_ref, x_ref, table_ref, *before, modes_ref, gram_ref, lhs, acc = refs
    sources, groups, rows, rank_rows, points = x_ref.shape
    step = pl.program_id(0)

    @pl.when(step == 0)
    def _():
        acc[...] = jnp.zeros_like(acc)
        for src in range(sources):
            half, place = divmod(src, sources // 2)
            for row in range(rows):
                for grp in range(groups):
                    start = ((half * rows + row) * groups + grp) * rank_rows
                    lhs[start : start + rank_rows, place * points : (place + 1) * points] = x_ref[
                        src, grp, row
                    ]

    span = groups * rank_rows
    values = lhs[...]
    halves = jnp.dot(values, table_ref[0], preferred_element_type=jnp.float32)
    halves += jnp.dot(values, table_ref[1], preferred_element_type=jnp.float32)
    col_ids = step * COL_TILE + lax.broadcasted_iota(jnp.int32, (1, COL_TILE), 1)
    wavenumber = jnp.where(col_ids < MMAX, col_ids, col_ids - MMAX + 1)
    turned = (1 - 2 * (wavenumber & 1)).astype(jnp.float32)
    spectra = halves[: rows * span] + turned * halves[rows * span :]
    tops, rests = [], []
    for row in range(rows):
        scaled = spectra[row * span : (row + 1) * span] * weight_ref[0, first_row + row]
        top = scaled.astype(jnp.bfloat16)
        rest = (scaled - top.astype(jnp.float32)).astype(jnp.bfloat16)
        modes_ref[row, :span] = top
        modes_ref[row, span:] = rest
        tops.append(top)
        rests.append(rest)
    top = jnp.concatenate(tops, axis=1)
    both = jnp.concatenate([top, jnp.concatenate(rests, axis=1)], axis=0)
    acc[...] += lax.dot_general(both, top, NT_DIMS, preferred_element_type=jnp.float32)

    @pl.when(step == pl.num_programs(0) - 1)
    def _():
        cross = acc[span:, :]
        gram = acc[:span, :] + (cross + cross.T)
        low = gram[rank_rows:, rank_rows:]
        low = jnp.concatenate([low[: rank_rows // 2], low[rank_rows // 2 :]], axis=1)
        packed = jnp.concatenate([gram[:rank_rows], low], axis=0)
        for ref in before:
            packed += ref[...]
        gram_ref[...] = packed


def spectra_and_gram(blocks, row_weight, table, first_row, *before):
    sources, groups, rows, rank_rows, points = blocks.shape
    _, half_lons, cols = table.shape
    span = groups * rank_rows
    packed = (rank_rows + rank_rows // 2, span)
    return pl.pallas_call(
        functools.partial(spectra_kernel, first_row=first_row),
        grid=(cols // COL_TILE,),
        in_specs=[
            pl.BlockSpec(memory_space=pltpu.SMEM),
            pl.BlockSpec(blocks.shape, lambda i: (0, 0, 0, 0, 0)),
            pl.BlockSpec((2, half_lons, COL_TILE), lambda i: (0, 0, i)),
            *[pl.BlockSpec(packed, lambda i: (0, 0)) for _ in before],
        ],
        out_specs=[
            pl.BlockSpec((rows, 2 * span, COL_TILE), lambda i: (0, 0, i)),
            pl.BlockSpec(packed, lambda i: (0, 0)),
        ],
        out_shape=[
            jax.ShapeDtypeStruct((rows, 2 * span, cols), jnp.bfloat16),
            jax.ShapeDtypeStruct(packed, jnp.float32),
        ],
        scratch_shapes=[
            pltpu.VMEM((2 * rows * span, half_lons), jnp.bfloat16),
            pltpu.VMEM((2 * span, span), jnp.float32),
        ],
        compiler_params=pltpu.CompilerParams(vmem_limit_bytes=VMEM_BYTES),
        cost_estimate=pl.CostEstimate(
            flops=8 * rows * span * half_lons * cols,
            bytes_accessed=2 * blocks.size + 4 * half_lons * cols + 4 * rows * span * cols,
            transcendentals=0,
        ),
    )(row_weight.reshape(1, -1), blocks, table, *before)


def dot_full(first, second, dims=(((1,), (0,)), ((), ()))):
    return lax.dot_general(
        first, second, dims, precision=highest, preferred_element_type=jnp.float32
    )


def eliminate(work, size, out_ref):
    height, width = work.shape
    for col in range(0, size, PIVOTS):
        base = col // 8 * 8
        lead = col - base
        rows = [work[lead + i : lead + i + 1, :] for i in range(PIVOTS)]
        cols = [
            jnp.broadcast_to(work[:, col + i : col + i + 1], (height - base, LANES)) for i in range(PIVOTS)
        ]
        update = None
        for i in range(PIVOTS):
            inverse = lax.rsqrt(cols[i][lead + i : lead + i + 1, :])
            wide = jnp.concatenate([inverse] * (width // LANES), axis=1)
            solved = rows[i] * wide
            out_ref[col + i : col + i + 1, :] = solved
            factor = cols[i] * inverse
            for k in range(i + 1, PIVOTS):
                share = factor[lead + k : lead + k + 1, :]
                cols[k] = cols[k] - factor * share
                rows[k] = rows[k] - solved * jnp.concatenate([share] * (width // LANES), axis=1)
            term = jnp.concatenate([factor] * (width // LANES), axis=1) * solved
            update = term if update is None else update + term
        following = (col + PIVOTS) // 8 * 8 - base
        work = work[following:] - update[following:]


def add_up(parts):
    while len(parts) > 1:
        parts = [parts[i] + parts[i + 1] for i in range(0, len(parts), 2)]
    return parts[0]


def unpacked(packed):
    span = packed.shape[1]
    rank = span // 2
    low = jnp.concatenate([packed[rank:, :rank], packed[rank:, rank:]], axis=0)
    square = jnp.concatenate(
        [packed[:rank], jnp.concatenate([jnp.zeros_like(low), low], axis=1)], axis=0
    )
    row_ids = lax.broadcasted_iota(jnp.int32, square.shape, 0)
    col_ids = lax.broadcasted_iota(jnp.int32, square.shape, 1)
    return jnp.where((row_ids >= rank) & (col_ids < rank), square.T, square)


def merge_kernel(*refs, split):
    *part_refs, test_ref, early_ref, late_ref, out_ref, mix_ref, first_ref, second_ref, held, sems = refs
    rank = test_ref.shape[0]
    row = pl.program_id(0)
    fetches = [
        pltpu.make_async_copy(early_ref, held.at[pl.ds(0, split)], sems.at[0]),
        pltpu.make_async_copy(late_ref, held.at[pl.ds(split, late_ref.shape[0])], sems.at[1]),
    ]

    @pl.when(row == 0)
    def _():
        for fetch in fetches:
            fetch.start()
        gram = unpacked(add_up([part[...] for part in part_refs]))
        test_t = test_ref[...]
        sketch = dot_full(gram, test_t, NT_DIMS)
        sketch_t = dot_full(test_t, gram)
        sketch_gram = dot_full(sketch_t, gram)
        power = dot_full(sketch_gram, sketch)
        power = 0.5 * (power + power.T)
        pad = jnp.zeros_like(power)
        eliminate(jnp.concatenate([power, pad, sketch_gram, sketch_t], axis=1), rank, first_ref)
        projected = first_ref[:, 2 * rank : 4 * rank]
        unmixed = first_ref[:, 4 * rank : 6 * rank]
        inner = dot_full(projected, projected, NT_DIMS)
        inner = 0.5 * (inner + inner.T)
        eliminate(jnp.concatenate([inner, pad], axis=1), rank, second_ref)
        upper = second_ref[:, :rank]
        col_ids = lax.broadcasted_iota(jnp.int32, upper.shape, 1)
        row_ids = lax.broadcasted_iota(jnp.int32, upper.shape, 0)
        mixing = dot_full(jnp.where(col_ids >= row_ids, upper, 0.0), unmixed)
        top = mixing.astype(jnp.bfloat16)
        rest = (mixing - top.astype(jnp.float32)).astype(jnp.bfloat16)
        mix_ref[:rank, : 2 * rank] = top
        mix_ref[:rank, 2 * rank :] = top
        mix_ref[rank:, : 2 * rank] = rest
        mix_ref[rank:, 2 * rank :] = jnp.zeros_like(rest)

        for fetch in fetches:
            fetch.wait()

    both = jnp.dot(mix_ref[...], held[row], preferred_element_type=jnp.float32)
    out_ref[...] = both[:rank] + both[rank:]


def merge_and_mix(gram_parts, test_matrix, early, late):
    split, height, cols = early.shape
    rows = split + late.shape[0]
    rank = test_matrix.shape[1]
    return pl.pallas_call(
        functools.partial(merge_kernel, split=split),
        grid=(rows,),
        in_specs=[
            *[pl.BlockSpec(part.shape, lambda i: (0, 0)) for part in gram_parts],
            pl.BlockSpec((rank, 2 * rank), lambda i: (0, 0)),
            pl.BlockSpec(memory_space=pl.ANY),
            pl.BlockSpec(memory_space=pl.ANY),
        ],
        out_specs=pl.BlockSpec((rank, cols), lambda i: (0, i)),
        out_shape=jax.ShapeDtypeStruct((rank, rows * cols), jnp.float32),
        scratch_shapes=[
            pltpu.VMEM((2 * rank, height), jnp.bfloat16),
            pltpu.VMEM((rank, 6 * rank), jnp.float32),
            pltpu.VMEM((rank, 2 * rank), jnp.float32),
            pltpu.VMEM((rows, height, cols), jnp.bfloat16),
            pltpu.SemaphoreType.DMA((2,)),
        ],
        compiler_params=pltpu.CompilerParams(vmem_limit_bytes=MERGE_VMEM_BYTES),
    )(*gram_parts, test_matrix.T, early, late)


def exchanged(array, axes, bits):
    count = lax.axis_size(axes)
    masks = [0]
    for bit in bits:
        masks += [mask | bit for mask in masks]
    return [array] + [
        lax.ppermute(array, axes, [(i, i ^ mask) for i in range(count)]) for mask in masks[1:]
    ]


def sum_parts(array, axes):
    bits = [1 << k for k in range(lax.axis_size(axes).bit_length() - 1)]
    parts = exchanged(array, axes, bits[:1])
    for group in (bits[1:2] + bits[-1:], *[bits[k : k + 2] for k in range(2, len(bits) - 1, 2)]):
        parts = exchanged(add_up(parts), axes, group)
    return parts


def local_pair(snapshots, test_matrix):
    points, rank_rows, total_rows = snapshots.shape
    lon_count, group_count = lax.axis_size("lon"), lax.axis_size("tm")
    dev_rows = total_rows // (lon_count * group_count)
    first_row = (lax.axis_index("lon") * group_count + lax.axis_index("tm")) * dev_rows
    row_weight = area_weight(first_row, dev_rows, NTH)
    table = split_table(NPH, MMAX)
    split = EARLY_ROWS * dev_rows // 8
    early, late = relayout(snapshots, lon_count * group_count, split)
    late, table = lax.optimization_barrier((late, table))
    modes, gram = [], []
    for first, part in ((0, early), (split, late)):
        blocks = lax.all_to_all(part, ("lon", "tm"), split_axis=0, concat_axis=0, tiled=True)
        blocks = blocks.reshape(lon_count, group_count, -1, rank_rows, points)
        spectra, *gram = spectra_and_gram(blocks, row_weight, table, first, *gram)
        modes.append(spectra)
    return merge_and_mix(sum_parts(gram[0], ("tm", "lon")), test_matrix, *modes)


def solution(mesh):
    lon_count, group_count = mesh.shape["lon"], mesh.shape["tm"]
    device_count = lon_count * group_count
    whole_rows = NTH % device_count == 0 and device_count & (device_count - 1) == 0
    return jax.shard_map(
        local_pair if group_count == 2 and whole_rows else local_tree,
        mesh=mesh,
        in_specs=(P("lon", "tm", None), P()),
        out_specs=P(None, ("lon", "tm")),
        check_vma=False,
    )
```

```python
import functools
import math

import jax
import jax.numpy as jnp
from jax import lax
from jax.experimental import pallas as pl
from jax.experimental.pallas import tpu as pltpu
from jax.sharding import PartitionSpec as P

NPH = 2048
MMAX = 640
NTH = 256
COL_TILE = 256
LANES = 128
PIVOTS = 4
SNAPSHOT_TILE = 16
EARLY_ROWS = 6
VMEM_BYTES = 50 * 2**20
RELAYOUT_VMEM_BYTES = 58 * 2**20


highest = lax.Precision.HIGHEST
NT_DIMS = (((1,), (1,)), ((), ()))


def swapped(array, axis, distance):
    return lax.ppermute(array, axis, [(i, i ^ 1 << distance) for i in range(lax.axis_size(axis))])


def matmul(first_op, second_op):
    return jnp.dot(first_op, second_op, precision=highest, preferred_element_type=jnp.float32)


def spectral_table(points, wave_count, row_count):
    lon_ids = jnp.arange(row_count, dtype=jnp.int32)
    col_ids = jnp.arange(2 * wave_count, dtype=jnp.int32)
    wavenumber = jnp.where(col_ids < wave_count, col_ids, col_ids - wave_count + 1)
    phase_index = lon_ids[:, None] * wavenumber[None, :] % points
    angles = 2.0 * math.pi / points * phase_index.astype(jnp.float32)
    trig_value = jnp.where(col_ids[None, :] < wave_count, jnp.cos(angles), jnp.sin(angles))
    col_scale = math.sqrt(2.0 / points) / jnp.sqrt(
        1.0 + 4.0 * wavenumber.astype(jnp.float32) / wave_count
    )
    return trig_value * col_scale[None, :]


def area_weight(start_row, row_count, total_rows):
    row_ids = start_row + jnp.arange(row_count, dtype=jnp.int32)
    colatitude = math.pi * (row_ids.astype(jnp.float32) + 0.5) / (2.0 * total_rows)
    return jnp.sqrt(jnp.sin(colatitude))


def merge_gram(gram_matrix, test_matrix):
    sketch = matmul(gram_matrix, test_matrix)
    sketch_gram = matmul(sketch.T, gram_matrix)
    power_gram = matmul(sketch_gram, sketch)
    power_gram = 0.5 * (power_gram + power_gram.T)
    chol_first = jnp.linalg.cholesky(power_gram)
    projected = lax.linalg.triangular_solve(chol_first, sketch_gram, left_side=True, lower=True)
    proj_gram = matmul(projected, projected.T)
    chol_second = jnp.linalg.cholesky(0.5 * (proj_gram + proj_gram.T))
    unmixed = lax.linalg.triangular_solve(chol_first, sketch.T, left_side=True, lower=True)
    mixing = matmul(chol_second.T, unmixed)
    return (mixing, matmul(chol_second.T, chol_second))


def block_gram(low_energy, cross_term, high_energy):
    top_rows = jnp.concatenate([low_energy, cross_term], axis=1)
    bottom_rows = jnp.concatenate([cross_term.T, high_energy], axis=1)
    return jnp.concatenate([top_rows, bottom_rows], axis=0)


def combine_pair(mixing, low_modes, high_modes):
    rank_rows = low_modes.shape[0]
    return matmul(mixing[:, :rank_rows], low_modes) + matmul(mixing[:, rank_rows:], high_modes)


def own_columns(modes_flat, group_index, group_count):
    col_count = modes_flat.shape[1] // group_count
    return lax.dynamic_slice_in_dim(modes_flat, group_index * col_count, col_count, 1)


def local_tree(snapshots, test_matrix):
    dev_rows = NTH // lax.axis_size("lon")
    dft_table = spectral_table(NPH, MMAX, NPH)
    row_weight = area_weight(lax.axis_index("lon") * dev_rows, dev_rows, NTH)
    spectra = jnp.einsum(
        "pst,pk->stk",
        lax.all_to_all(snapshots, "lon", split_axis=2, concat_axis=0, tiled=True).astype(
            jnp.float32
        ),
        dft_table,
        precision=highest,
    )
    spectra = spectra * row_weight[None, :, None]
    rank_rows = spectra.shape[0]
    modes_now = spectra.reshape(rank_rows, -1)
    levels_count = lax.axis_size("tm").bit_length() - 1
    group_index = lax.axis_index("tm")
    group_count = lax.axis_size("tm")
    energy = lax.psum(matmul(modes_now, modes_now.T), "lon")
    start_level = 0
    for tree_level in range(start_level, levels_count):
        partner_modes, partner_energy = swapped((modes_now, energy), "tm", tree_level)
        is_upper = group_index // 2**tree_level % 2 == 1
        low_modes = jnp.where(is_upper, partner_modes, modes_now)
        high_modes = jnp.where(is_upper, modes_now, partner_modes)
        low_energy = jnp.where(is_upper, partner_energy, energy)
        high_energy = jnp.where(is_upper, energy, partner_energy)
        cross_term = lax.psum(matmul(low_modes, high_modes.T), "lon")
        mixing, energy = merge_gram(block_gram(low_energy, cross_term, high_energy), test_matrix)
        modes_now = combine_pair(mixing, low_modes, high_modes)
    return own_columns(modes_now, group_index, group_count)


def split_table(points, wave_count):
    table = spectral_table(points, wave_count, points // 2)
    table = table.reshape(points // 2, -1, COL_TILE).transpose(1, 0, 2)
    high = lax.reduce_precision(table, 8, 7)
    return jnp.stack([high.astype(jnp.bfloat16), (table - high).astype(jnp.bfloat16)], axis=1)


def relayout_kernel(x_ref, first_ref, last_ref):
    points, some, total = x_ref.shape
    devices, split = first_ref.shape[:2]
    by_snapshot = jnp.transpose(x_ref[...], (1, 0, 2))
    turned = jnp.stack([by_snapshot[i].T for i in range(some)], axis=0)
    rows = jnp.transpose(turned, (1, 0, 2)).reshape(devices, total // devices, some, points)
    first_ref[...] = rows[:, :split]
    last_ref[...] = rows[:, split:]


def relayout(snapshots, devices, split):
    points, rank_rows, total = snapshots.shape
    some = SNAPSHOT_TILE
    cuts = (split, total // devices - split)
    return pl.pallas_call(
        relayout_kernel,
        grid=(rank_rows // some,),
        in_specs=[pl.BlockSpec((points, some, total), lambda i: (0, i, 0))],
        out_specs=[pl.BlockSpec((devices, cut, some, points), lambda i: (0, 0, i, 0)) for cut in cuts],
        out_shape=[
            jax.ShapeDtypeStruct((devices, cut, rank_rows, points), snapshots.dtype) for cut in cuts
        ],
        compiler_params=pltpu.CompilerParams(vmem_limit_bytes=RELAYOUT_VMEM_BYTES),
    )(snapshots)


def spectra_kernel(*refs, first_row):
    weight_ref, x_ref, table_ref, *before, modes_ref, gram_ref, lhs, acc, held, sems = refs
    sources, groups, rows, rank_rows, points = x_ref.shape
    tiles = table_ref.shape[0]
    span = groups * rank_rows

    def fetch(step):
        return pltpu.make_async_copy(table_ref.at[step], held.at[step], sems.at[step])

    for step in range(tiles):
        fetch(step).start()
    acc[...] = jnp.zeros_like(acc)
    for src in range(sources):
        half, place = divmod(src, sources // 2)
        for row in range(rows):
            for grp in range(groups):
                start = ((half * rows + row) * groups + grp) * rank_rows
                lhs[start : start + rank_rows, place * points : (place + 1) * points] = x_ref[
                    src, grp, row
                ]

    @pl.loop(0, tiles)
    def _(step):
        fetch(step).wait()
        tile = pl.ds(pl.multiple_of(step * COL_TILE, COL_TILE), COL_TILE)
        values = lhs[...]
        halves = jnp.dot(values, held[step, 0], preferred_element_type=jnp.float32)
        halves += jnp.dot(values, held[step, 1], preferred_element_type=jnp.float32)
        col_ids = step * COL_TILE + lax.broadcasted_iota(jnp.int32, (1, COL_TILE), 1)
        wavenumber = jnp.where(col_ids < MMAX, col_ids, col_ids - MMAX + 1)
        turned = (1 - 2 * (wavenumber & 1)).astype(jnp.float32)
        spectra = halves[: rows * span] + turned * halves[rows * span :]
        tops, rests = [], []
        for row in range(rows):
            scaled = spectra[row * span : (row + 1) * span] * weight_ref[0, first_row + row]
            top = scaled.astype(jnp.bfloat16)
            rest = (scaled - top.astype(jnp.float32)).astype(jnp.bfloat16)
            modes_ref[row, :span, tile] = top
            modes_ref[row, span:, tile] = rest
            tops.append(top)
            rests.append(rest)
        top = jnp.concatenate(tops, axis=1)
        both = jnp.concatenate([top, jnp.concatenate(rests, axis=1)], axis=0)
        acc[...] += lax.dot_general(both, top, NT_DIMS, preferred_element_type=jnp.float32)

    cross = acc[span:, :]
    gram = acc[:span, :] + (cross + cross.T)
    low = gram[rank_rows:, rank_rows:]
    low = jnp.concatenate([low[: rank_rows // 2], low[rank_rows // 2 :]], axis=1)
    packed = jnp.concatenate([gram[:rank_rows], low], axis=0)
    for ref in before:
        packed += ref[...]
    gram_ref[...] = packed


def spectra_and_gram(blocks, row_weight, table, first_row, *before):
    sources, groups, rows, rank_rows, points = blocks.shape
    tiles, _, half_lons, _ = table.shape
    cols = tiles * COL_TILE
    span = groups * rank_rows
    packed = (rank_rows + rank_rows // 2, span)
    return pl.pallas_call(
        functools.partial(spectra_kernel, first_row=first_row),
        in_specs=[
            pl.BlockSpec(memory_space=pltpu.SMEM),
            pl.BlockSpec(memory_space=pltpu.VMEM),
            pl.BlockSpec(memory_space=pl.ANY),
            *[pl.BlockSpec(memory_space=pltpu.VMEM) for _ in before],
        ],
        out_specs=[pl.BlockSpec(memory_space=pltpu.VMEM)] * 2,
        out_shape=[
            jax.ShapeDtypeStruct((rows, 2 * span, cols), jnp.bfloat16),
            jax.ShapeDtypeStruct(packed, jnp.float32),
        ],
        scratch_shapes=[
            pltpu.VMEM((2 * rows * span, half_lons), jnp.bfloat16),
            pltpu.VMEM((2 * span, span), jnp.float32),
            pltpu.VMEM(table.shape, table.dtype),
            pltpu.SemaphoreType.DMA((tiles,)),
        ],
        compiler_params=pltpu.CompilerParams(vmem_limit_bytes=VMEM_BYTES),
        cost_estimate=pl.CostEstimate(
            flops=8 * rows * span * half_lons * cols,
            bytes_accessed=2 * blocks.size + 4 * half_lons * cols + 4 * rows * span * cols,
            transcendentals=0,
        ),
    )(row_weight.reshape(1, -1), blocks, table, *before)


def dot_full(first, second, dims=(((1,), (0,)), ((), ()))):
    return lax.dot_general(
        first, second, dims, precision=highest, preferred_element_type=jnp.float32
    )


def eliminate(work, size, out_ref):
    height, width = work.shape
    for col in range(0, size, PIVOTS):
        base = col // 8 * 8
        lead = col - base
        rows = [work[lead + i : lead + i + 1, :] for i in range(PIVOTS)]
        cols = [
            jnp.broadcast_to(work[:, col + i : col + i + 1], (height - base, LANES)) for i in range(PIVOTS)
        ]
        update = None
        for i in range(PIVOTS):
            inverse = lax.rsqrt(cols[i][lead + i : lead + i + 1, :])
            wide = jnp.concatenate([inverse] * (width // LANES), axis=1)
            solved = rows[i] * wide
            out_ref[col + i : col + i + 1, :] = solved
            factor = cols[i] * inverse
            for k in range(i + 1, PIVOTS):
                share = factor[lead + k : lead + k + 1, :]
                cols[k] = cols[k] - factor * share
                rows[k] = rows[k] - solved * jnp.concatenate([share] * (width // LANES), axis=1)
            term = jnp.concatenate([factor] * (width // LANES), axis=1) * solved
            update = term if update is None else update + term
        following = (col + PIVOTS) // 8 * 8 - base
        work = work[following:] - update[following:]


def add_up(parts):
    while len(parts) > 1:
        parts = [parts[i] + parts[i + 1] for i in range(0, len(parts), 2)]
    return parts[0]


def unpacked(packed):
    span = packed.shape[1]
    rank = span // 2
    low = jnp.concatenate([packed[rank:, :rank], packed[rank:, rank:]], axis=0)
    square = jnp.concatenate(
        [packed[:rank], jnp.concatenate([jnp.zeros_like(low), low], axis=1)], axis=0
    )
    row_ids = lax.broadcasted_iota(jnp.int32, square.shape, 0)
    col_ids = lax.broadcasted_iota(jnp.int32, square.shape, 1)
    return jnp.where((row_ids >= rank) & (col_ids < rank), square.T, square)


def merge_kernel(*refs, split):
    *part_refs, test_ref, early_ref, late_ref, out_ref, mix_ref, first_ref, second_ref, held, sems = refs
    rank = test_ref.shape[0]
    row = pl.program_id(0)
    fetches = [
        pltpu.make_async_copy(early_ref, held.at[pl.ds(0, split)], sems.at[0]),
        pltpu.make_async_copy(late_ref, held.at[pl.ds(split, late_ref.shape[0])], sems.at[1]),
    ]

    @pl.when(row == 0)
    def _():
        for fetch in fetches:
            fetch.start()
        gram = unpacked(add_up([part[...] for part in part_refs]))
        test_t = test_ref[...]
        sketch = dot_full(gram, test_t, NT_DIMS)
        sketch_t = dot_full(test_t, gram)
        sketch_gram = dot_full(sketch_t, gram)
        power = dot_full(sketch_gram, sketch)
        power = 0.5 * (power + power.T)
        pad = jnp.zeros_like(power)
        eliminate(jnp.concatenate([power, pad, sketch_gram, sketch_t], axis=1), rank, first_ref)
        projected = first_ref[:, 2 * rank : 4 * rank]
        unmixed = first_ref[:, 4 * rank : 6 * rank]
        inner = dot_full(projected, projected, NT_DIMS)
        inner = 0.5 * (inner + inner.T)
        eliminate(jnp.concatenate([inner, pad], axis=1), rank, second_ref)
        upper = second_ref[:, :rank]
        col_ids = lax.broadcasted_iota(jnp.int32, upper.shape, 1)
        row_ids = lax.broadcasted_iota(jnp.int32, upper.shape, 0)
        mixing = dot_full(jnp.where(col_ids >= row_ids, upper, 0.0), unmixed)
        top = mixing.astype(jnp.bfloat16)
        rest = (mixing - top.astype(jnp.float32)).astype(jnp.bfloat16)
        mix_ref[:rank, : 2 * rank] = top
        mix_ref[:rank, 2 * rank :] = top
        mix_ref[rank:, : 2 * rank] = rest
        mix_ref[rank:, 2 * rank :] = jnp.zeros_like(rest)

        for fetch in fetches:
            fetch.wait()

    both = jnp.dot(mix_ref[...], held[row], preferred_element_type=jnp.float32)
    out_ref[...] = both[:rank] + both[rank:]


def merge_and_mix(gram_parts, test_matrix, early, late):
    split, height, cols = early.shape
    rows = split + late.shape[0]
    rank = test_matrix.shape[1]
    return pl.pallas_call(
        functools.partial(merge_kernel, split=split),
        grid=(rows,),
        in_specs=[
            *[pl.BlockSpec(part.shape, lambda i: (0, 0)) for part in gram_parts],
            pl.BlockSpec((rank, 2 * rank), lambda i: (0, 0)),
            pl.BlockSpec(memory_space=pl.ANY),
            pl.BlockSpec(memory_space=pl.ANY),
        ],
        out_specs=pl.BlockSpec((rank, cols), lambda i: (0, i)),
        out_shape=jax.ShapeDtypeStruct((rank, rows * cols), jnp.float32),
        scratch_shapes=[
            pltpu.VMEM((2 * rank, height), jnp.bfloat16),
            pltpu.VMEM((rank, 6 * rank), jnp.float32),
            pltpu.VMEM((rank, 2 * rank), jnp.float32),
            pltpu.VMEM((rows, height, cols), jnp.bfloat16),
            pltpu.SemaphoreType.DMA((2,)),
        ],
        compiler_params=pltpu.CompilerParams(vmem_limit_bytes=VMEM_BYTES),
    )(*gram_parts, test_matrix.T, early, late)


def exchanged(array, axes, bits):
    count = lax.axis_size(axes)
    masks = [0]
    for bit in bits:
        masks += [mask | bit for mask in masks]
    return [array] + [
        lax.ppermute(array, axes, [(i, i ^ mask) for i in range(count)]) for mask in masks[1:]
    ]


def sum_parts(array, axes):
    bits = [1 << k for k in range(lax.axis_size(axes).bit_length() - 1)]
    parts = exchanged(array, axes, bits[:1])
    for group in (bits[1:2] + bits[-1:], *[bits[k : k + 2] for k in range(2, len(bits) - 1, 2)]):
        parts = exchanged(add_up(parts), axes, group)
    return parts


def local_pair(snapshots, test_matrix):
    points, rank_rows, total_rows = snapshots.shape
    lon_count, group_count = lax.axis_size("lon"), lax.axis_size("tm")
    dev_rows = total_rows // (lon_count * group_count)
    first_row = (lax.axis_index("lon") * group_count + lax.axis_index("tm")) * dev_rows
    row_weight = area_weight(first_row, dev_rows, NTH)
    table = split_table(NPH, MMAX)
    split = EARLY_ROWS * dev_rows // 8
    early, late = relayout(snapshots, lon_count * group_count, split)
    late, table = lax.optimization_barrier((late, table))
    modes, gram = [], []
    for first, part in ((0, early), (split, late)):
        blocks = lax.all_to_all(part, ("lon", "tm"), split_axis=0, concat_axis=0, tiled=True)
        blocks = blocks.reshape(lon_count, group_count, -1, rank_rows, points)
        spectra, *gram = spectra_and_gram(blocks, row_weight, table, first, *gram)
        modes.append(spectra)
    return merge_and_mix(sum_parts(gram[0], ("tm", "lon")), test_matrix, *modes)


def solution(mesh):
    lon_count, group_count = mesh.shape["lon"], mesh.shape["tm"]
    device_count = lon_count * group_count
    whole_rows = NTH % device_count == 0 and device_count & (device_count - 1) == 0
    return jax.shard_map(
        local_pair if group_count == 2 and whole_rows else local_tree,
        mesh=mesh,
        in_specs=(P("lon", "tm", None), P()),
        out_specs=P(None, ("lon", "tm")),
        check_vma=False,
    )
```

```python
import functools
import math

import jax
import jax.numpy as jnp
from jax import lax
from jax.experimental import pallas as pl
from jax.experimental.pallas import tpu as pltpu
from jax.sharding import PartitionSpec as P

NPH = 2048
MMAX = 640
NTH = 256
COL_TILE = 256
LANES = 128
PIVOTS = 4
SNAPSHOT_TILE = 16
EARLY_ROWS = 6
VMEM_BYTES = 50 * 2**20
RELAYOUT_VMEM_BYTES = 58 * 2**20


highest = lax.Precision.HIGHEST
NT_DIMS = (((1,), (1,)), ((), ()))


def swapped(array, axis, distance):
    return lax.ppermute(array, axis, [(i, i ^ 1 << distance) for i in range(lax.axis_size(axis))])


def matmul(first_op, second_op):
    return jnp.dot(first_op, second_op, precision=highest, preferred_element_type=jnp.float32)


def spectral_table(points, wave_count, row_count):
    lon_ids = jnp.arange(row_count, dtype=jnp.int32)
    col_ids = jnp.arange(2 * wave_count, dtype=jnp.int32)
    wavenumber = jnp.where(col_ids < wave_count, col_ids, col_ids - wave_count + 1)
    phase_index = lon_ids[:, None] * wavenumber[None, :] % points
    angles = 2.0 * math.pi / points * phase_index.astype(jnp.float32)
    trig_value = jnp.where(col_ids[None, :] < wave_count, jnp.cos(angles), jnp.sin(angles))
    col_scale = math.sqrt(2.0 / points) / jnp.sqrt(
        1.0 + 4.0 * wavenumber.astype(jnp.float32) / wave_count
    )
    return trig_value * col_scale[None, :]


def area_weight(start_row, row_count, total_rows):
    row_ids = start_row + jnp.arange(row_count, dtype=jnp.int32)
    colatitude = math.pi * (row_ids.astype(jnp.float32) + 0.5) / (2.0 * total_rows)
    return jnp.sqrt(jnp.sin(colatitude))


def merge_gram(gram_matrix, test_matrix):
    sketch = matmul(gram_matrix, test_matrix)
    sketch_gram = matmul(sketch.T, gram_matrix)
    power_gram = matmul(sketch_gram, sketch)
    power_gram = 0.5 * (power_gram + power_gram.T)
    chol_first = jnp.linalg.cholesky(power_gram)
    projected = lax.linalg.triangular_solve(chol_first, sketch_gram, left_side=True, lower=True)
    proj_gram = matmul(projected, projected.T)
    chol_second = jnp.linalg.cholesky(0.5 * (proj_gram + proj_gram.T))
    unmixed = lax.linalg.triangular_solve(chol_first, sketch.T, left_side=True, lower=True)
    mixing = matmul(chol_second.T, unmixed)
    return (mixing, matmul(chol_second.T, chol_second))


def block_gram(low_energy, cross_term, high_energy):
    top_rows = jnp.concatenate([low_energy, cross_term], axis=1)
    bottom_rows = jnp.concatenate([cross_term.T, high_energy], axis=1)
    return jnp.concatenate([top_rows, bottom_rows], axis=0)


def combine_pair(mixing, low_modes, high_modes):
    rank_rows = low_modes.shape[0]
    return matmul(mixing[:, :rank_rows], low_modes) + matmul(mixing[:, rank_rows:], high_modes)


def own_columns(modes_flat, group_index, group_count):
    col_count = modes_flat.shape[1] // group_count
    return lax.dynamic_slice_in_dim(modes_flat, group_index * col_count, col_count, 1)


def local_tree(snapshots, test_matrix):
    dev_rows = NTH // lax.axis_size("lon")
    dft_table = spectral_table(NPH, MMAX, NPH)
    row_weight = area_weight(lax.axis_index("lon") * dev_rows, dev_rows, NTH)
    spectra = jnp.einsum(
        "pst,pk->stk",
        lax.all_to_all(snapshots, "lon", split_axis=2, concat_axis=0, tiled=True).astype(
            jnp.float32
        ),
        dft_table,
        precision=highest,
    )
    spectra = spectra * row_weight[None, :, None]
    rank_rows = spectra.shape[0]
    modes_now = spectra.reshape(rank_rows, -1)
    levels_count = lax.axis_size("tm").bit_length() - 1
    group_index = lax.axis_index("tm")
    group_count = lax.axis_size("tm")
    energy = lax.psum(matmul(modes_now, modes_now.T), "lon")
    start_level = 0
    for tree_level in range(start_level, levels_count):
        partner_modes, partner_energy = swapped((modes_now, energy), "tm", tree_level)
        is_upper = group_index // 2**tree_level % 2 == 1
        low_modes = jnp.where(is_upper, partner_modes, modes_now)
        high_modes = jnp.where(is_upper, modes_now, partner_modes)
        low_energy = jnp.where(is_upper, partner_energy, energy)
        high_energy = jnp.where(is_upper, energy, partner_energy)
        cross_term = lax.psum(matmul(low_modes, high_modes.T), "lon")
        mixing, energy = merge_gram(block_gram(low_energy, cross_term, high_energy), test_matrix)
        modes_now = combine_pair(mixing, low_modes, high_modes)
    return own_columns(modes_now, group_index, group_count)


def split_table(points, wave_count):
    table = spectral_table(points, wave_count, points // 2)
    table = table.reshape(points // 2, -1, COL_TILE).transpose(1, 0, 2)
    high = lax.reduce_precision(table, 8, 7)
    return jnp.stack([high.astype(jnp.bfloat16), (table - high).astype(jnp.bfloat16)], axis=1)


def ids(shape):
    return lax.broadcasted_iota(jnp.int32, shape, 0), lax.broadcasted_iota(jnp.int32, shape, 1)


def packed_gram(gram):
    rank = gram.shape[0] // 2
    high, cross, low = gram[:rank, :rank], gram[:rank, rank:], gram[rank:, rank:]
    row_ids, col_ids = ids(high.shape)
    both = jnp.where(col_ids >= row_ids, high, low)
    diagonal = jnp.sum(jnp.where(col_ids == row_ids, low, 0.0), axis=0, keepdims=True)
    diagonal = jnp.broadcast_to(jnp.concatenate([diagonal, diagonal], axis=1), (8, 2 * rank))
    return jnp.concatenate([jnp.concatenate([both, cross], axis=1), diagonal], axis=0)


def unpacked_gram(packed):
    rank = packed.shape[1] // 2
    both, cross, diagonal = packed[:rank, :rank], packed[:rank, rank:], packed[rank : rank + 1, :rank]
    row_ids, col_ids = ids(both.shape)
    turned = both.T
    high = jnp.where(col_ids >= row_ids, both, turned)
    low = jnp.where(col_ids < row_ids, both, turned)
    low = jnp.where(col_ids == row_ids, jnp.broadcast_to(diagonal, low.shape), low)
    top = jnp.concatenate([high, cross], axis=1)
    return jnp.concatenate([top, jnp.concatenate([cross.T, low], axis=1)], axis=0)


def relayout_kernel(x_ref, first_ref, last_ref):
    points, some, total = x_ref.shape
    devices, split = first_ref.shape[:2]
    by_snapshot = jnp.transpose(x_ref[...], (1, 0, 2))
    turned = jnp.stack([by_snapshot[i].T for i in range(some)], axis=0)
    rows = jnp.transpose(turned, (1, 0, 2)).reshape(devices, total // devices, some, points)
    first_ref[...] = rows[:, :split]
    last_ref[...] = rows[:, split:]


def relayout(snapshots, devices, split):
    points, rank_rows, total = snapshots.shape
    some = SNAPSHOT_TILE
    cuts = (split, total // devices - split)
    return pl.pallas_call(
        relayout_kernel,
        grid=(rank_rows // some,),
        in_specs=[pl.BlockSpec((points, some, total), lambda i: (0, i, 0))],
        out_specs=[pl.BlockSpec((devices, cut, some, points), lambda i: (0, 0, i, 0)) for cut in cuts],
        out_shape=[
            jax.ShapeDtypeStruct((devices, cut, rank_rows, points), snapshots.dtype) for cut in cuts
        ],
        compiler_params=pltpu.CompilerParams(vmem_limit_bytes=RELAYOUT_VMEM_BYTES),
    )(snapshots)


def spectra_kernel(*refs, first_row):
    weight_ref, x_ref, table_ref, *before, modes_ref, gram_ref, lhs, acc, held, sems, own, own_sems = refs
    sources, groups, rows, rank_rows, points = x_ref.shape
    tiles = table_ref.shape[0]
    span = groups * rank_rows

    def fetch(step):
        return pltpu.make_async_copy(table_ref.at[step], held.at[step], sems.at[step])

    takes = []
    for half in range(2):
        part = pl.ds(half * sources // 2, sources // 2)
        takes.append(pltpu.make_async_copy(x_ref.at[part], own.at[part], own_sems.at[half]))
    for take in takes:
        take.start()
    fetch(0).start()
    acc[...] = jnp.zeros_like(acc)
    for src in range(sources):
        half, place = divmod(src, sources // 2)
        if place == 0:
            takes[half].wait()
            for step in range(1 + half, tiles, 2):
                fetch(step).start()
        for row in range(rows):
            for grp in range(groups):
                start = ((half * rows + row) * groups + grp) * rank_rows
                lhs[start : start + rank_rows, place * points : (place + 1) * points] = own[
                    src, grp, row
                ]

    @pl.loop(0, tiles)
    def _(step):
        fetch(step).wait()
        tile = pl.ds(pl.multiple_of(step * COL_TILE, COL_TILE), COL_TILE)
        values = lhs[...]
        halves = jnp.dot(values, held[step, 0], preferred_element_type=jnp.float32)
        halves += jnp.dot(values, held[step, 1], preferred_element_type=jnp.float32)
        col_ids = step * COL_TILE + lax.broadcasted_iota(jnp.int32, (1, COL_TILE), 1)
        wavenumber = jnp.where(col_ids < MMAX, col_ids, col_ids - MMAX + 1)
        turned = (1 - 2 * (wavenumber & 1)).astype(jnp.float32)
        spectra = halves[: rows * span] + turned * halves[rows * span :]
        tops, rests = [], []
        for row in range(rows):
            scaled = spectra[row * span : (row + 1) * span] * weight_ref[0, first_row + row]
            top = scaled.astype(jnp.bfloat16)
            rest = (scaled - top.astype(jnp.float32)).astype(jnp.bfloat16)
            modes_ref[row, :span, tile] = top
            modes_ref[row, span:, tile] = rest
            tops.append(top)
            rests.append(rest)
        top = jnp.concatenate(tops, axis=1)
        both = jnp.concatenate([top, jnp.concatenate(rests, axis=1)], axis=0)
        acc[...] += lax.dot_general(both, top, NT_DIMS, preferred_element_type=jnp.float32)

    cross = acc[span:, :]
    gram = acc[:span, :] + (cross + cross.T)
    packed = packed_gram(gram)
    for ref in before:
        packed += ref[...]
    gram_ref[...] = packed


def spectra_and_gram(blocks, row_weight, table, first_row, *before):
    sources, groups, rows, rank_rows, points = blocks.shape
    tiles, _, half_lons, _ = table.shape
    cols = tiles * COL_TILE
    span = groups * rank_rows
    packed = (rank_rows + 8, span)
    return pl.pallas_call(
        functools.partial(spectra_kernel, first_row=first_row),
        in_specs=[
            pl.BlockSpec(memory_space=pltpu.SMEM),
            pl.BlockSpec(memory_space=pl.ANY),
            pl.BlockSpec(memory_space=pl.ANY),
            *[pl.BlockSpec(memory_space=pltpu.VMEM) for _ in before],
        ],
        out_specs=[pl.BlockSpec(memory_space=pltpu.VMEM)] * 2,
        out_shape=[
            jax.ShapeDtypeStruct((rows, 2 * span, cols), jnp.bfloat16),
            jax.ShapeDtypeStruct(packed, jnp.float32),
        ],
        scratch_shapes=[
            pltpu.VMEM((2 * rows * span, half_lons), jnp.bfloat16),
            pltpu.VMEM((2 * span, span), jnp.float32),
            pltpu.VMEM(table.shape, table.dtype),
            pltpu.SemaphoreType.DMA((tiles,)),
            pltpu.VMEM(blocks.shape, blocks.dtype),
            pltpu.SemaphoreType.DMA((2,)),
        ],
        compiler_params=pltpu.CompilerParams(vmem_limit_bytes=VMEM_BYTES),
        cost_estimate=pl.CostEstimate(
            flops=8 * rows * span * half_lons * cols,
            bytes_accessed=2 * blocks.size + 4 * half_lons * cols + 4 * rows * span * cols,
            transcendentals=0,
        ),
    )(row_weight.reshape(1, -1), blocks, table, *before)


def dot_full(first, second, dims=(((1,), (0,)), ((), ()))):
    return lax.dot_general(
        first, second, dims, precision=highest, preferred_element_type=jnp.float32
    )


def eliminate(work, size, out_ref):
    height, width = work.shape
    for col in range(0, size, PIVOTS):
        base = col // 8 * 8
        lead = col - base
        rows = [work[lead + i : lead + i + 1, :] for i in range(PIVOTS)]
        cols = [
            jnp.broadcast_to(work[:, col + i : col + i + 1], (height - base, LANES)) for i in range(PIVOTS)
        ]
        update = None
        for i in range(PIVOTS):
            inverse = lax.rsqrt(cols[i][lead + i : lead + i + 1, :])
            wide = jnp.concatenate([inverse] * (width // LANES), axis=1)
            solved = rows[i] * wide
            out_ref[col + i : col + i + 1, :] = solved
            factor = cols[i] * inverse
            for k in range(i + 1, PIVOTS):
                share = factor[lead + k : lead + k + 1, :]
                cols[k] = cols[k] - factor * share
                rows[k] = rows[k] - solved * jnp.concatenate([share] * (width // LANES), axis=1)
            term = jnp.concatenate([factor] * (width // LANES), axis=1) * solved
            update = term if update is None else update + term
        following = (col + PIVOTS) // 8 * 8 - base
        work = work[following:] - update[following:]


def add_up(parts):
    while len(parts) > 1:
        parts = [parts[i] + parts[i + 1] for i in range(0, len(parts), 2)]
    return parts[0]


def merge_kernel(*refs, split):
    *part_refs, test_ref, early_ref, late_ref, out_ref, mix_ref, first_ref, second_ref, held, sems = refs
    rank = test_ref.shape[0]
    row = pl.program_id(0)
    fetches = [
        pltpu.make_async_copy(early_ref, held.at[pl.ds(0, split)], sems.at[0]),
        pltpu.make_async_copy(late_ref, held.at[pl.ds(split, late_ref.shape[0])], sems.at[1]),
    ]

    @pl.when(row == 0)
    def _():
        for fetch in fetches:
            fetch.start()
        gram = unpacked_gram(add_up([part[...] for part in part_refs]))
        test_t = test_ref[...]
        sketch = dot_full(gram, test_t, NT_DIMS)
        sketch_t = dot_full(test_t, gram)
        sketch_gram = dot_full(sketch_t, gram)
        power = dot_full(sketch_gram, sketch)
        power = 0.5 * (power + power.T)
        pad = jnp.zeros_like(power)
        eliminate(jnp.concatenate([power, pad, sketch_gram, sketch_t], axis=1), rank, first_ref)
        projected = first_ref[:, 2 * rank : 4 * rank]
        unmixed = first_ref[:, 4 * rank : 6 * rank]
        inner = dot_full(projected, projected, NT_DIMS)
        inner = 0.5 * (inner + inner.T)
        eliminate(jnp.concatenate([inner, pad], axis=1), rank, second_ref)
        upper = second_ref[:, :rank]
        row_ids, col_ids = ids(upper.shape)
        mixing = dot_full(jnp.where(col_ids >= row_ids, upper, 0.0), unmixed)
        top = mixing.astype(jnp.bfloat16)
        rest = (mixing - top.astype(jnp.float32)).astype(jnp.bfloat16)
        mix_ref[:rank, : 2 * rank] = top
        mix_ref[:rank, 2 * rank :] = top
        mix_ref[rank:, : 2 * rank] = rest
        mix_ref[rank:, 2 * rank :] = jnp.zeros_like(rest)

        for fetch in fetches:
            fetch.wait()

    both = jnp.dot(mix_ref[...], held[row], preferred_element_type=jnp.float32)
    out_ref[...] = both[:rank] + both[rank:]


def merge_and_mix(gram_parts, test_matrix, early, late):
    split, height, cols = early.shape
    rows = split + late.shape[0]
    rank = test_matrix.shape[1]
    return pl.pallas_call(
        functools.partial(merge_kernel, split=split),
        grid=(rows,),
        in_specs=[
            *[pl.BlockSpec(part.shape, lambda i: (0, 0)) for part in gram_parts],
            pl.BlockSpec((rank, 2 * rank), lambda i: (0, 0)),
            pl.BlockSpec(memory_space=pl.ANY),
            pl.BlockSpec(memory_space=pl.ANY),
        ],
        out_specs=pl.BlockSpec((rank, cols), lambda i: (0, i)),
        out_shape=jax.ShapeDtypeStruct((rank, rows * cols), jnp.float32),
        scratch_shapes=[
            pltpu.VMEM((2 * rank, height), jnp.bfloat16),
            pltpu.VMEM((rank, 6 * rank), jnp.float32),
            pltpu.VMEM((rank, 2 * rank), jnp.float32),
            pltpu.VMEM((rows, height, cols), jnp.bfloat16),
            pltpu.SemaphoreType.DMA((2,)),
        ],
        compiler_params=pltpu.CompilerParams(vmem_limit_bytes=VMEM_BYTES),
    )(*gram_parts, test_matrix.T, early, late)


def exchanged(array, axes, bits):
    count = lax.axis_size(axes)
    masks = [0]
    for bit in bits:
        masks += [mask | bit for mask in masks]
    return [array] + [
        lax.ppermute(array, axes, [(i, i ^ mask) for i in range(count)]) for mask in masks[1:]
    ]


def sum_parts(array, axes):
    bits = [1 << k for k in range(lax.axis_size(axes).bit_length() - 1)]
    parts = exchanged(array, axes, bits[:1])
    for group in (bits[1:2] + bits[-1:], *[bits[k : k + 2] for k in range(2, len(bits) - 1, 2)]):
        parts = exchanged(add_up(parts), axes, group)
    return parts


def local_pair(snapshots, test_matrix):
    points, rank_rows, total_rows = snapshots.shape
    lon_count, group_count = lax.axis_size("lon"), lax.axis_size("tm")
    dev_rows = total_rows // (lon_count * group_count)
    first_row = (lax.axis_index("lon") * group_count + lax.axis_index("tm")) * dev_rows
    row_weight = area_weight(first_row, dev_rows, NTH)
    table = split_table(NPH, MMAX)
    split = EARLY_ROWS * dev_rows // 8
    early, late = relayout(snapshots, lon_count * group_count, split)
    late, table = lax.optimization_barrier((late, table))
    modes, gram = [], []
    for first, part in ((0, early), (split, late)):
        blocks = lax.all_to_all(part, ("lon", "tm"), split_axis=0, concat_axis=0, tiled=True)
        blocks = blocks.reshape(lon_count, group_count, -1, rank_rows, points)
        spectra, *gram = spectra_and_gram(blocks, row_weight, table, first, *gram)
        modes.append(spectra)
    return merge_and_mix(sum_parts(gram[0], ("tm", "lon")), test_matrix, *modes)


def solution(mesh):
    lon_count, group_count = mesh.shape["lon"], mesh.shape["tm"]
    device_count = lon_count * group_count
    whole_rows = NTH % device_count == 0 and device_count & (device_count - 1) == 0
    return jax.shard_map(
        local_pair if group_count == 2 and whole_rows else local_tree,
        mesh=mesh,
        in_specs=(P("lon", "tm", None), P()),
        out_specs=P(None, ("lon", "tm")),
        check_vma=False,
    )
```

```python
import functools
import math

import jax
import jax.numpy as jnp
from jax import lax
from jax.experimental import pallas as pl
from jax.experimental.pallas import tpu as pltpu
from jax.sharding import PartitionSpec as P

NPH = 2048
MMAX = 640
NTH = 256
COL_TILE = 256
LANES = 128
PIVOTS = 16
SNAPSHOT_TILE = 16
EARLY_ROWS = 6
VMEM_BYTES = 50 * 2**20
RELAYOUT_VMEM_BYTES = 58 * 2**20


highest = lax.Precision.HIGHEST
NT_DIMS = (((1,), (1,)), ((), ()))


def swapped(array, axis, distance):
    return lax.ppermute(array, axis, [(i, i ^ 1 << distance) for i in range(lax.axis_size(axis))])


def matmul(first_op, second_op):
    return jnp.dot(first_op, second_op, precision=highest, preferred_element_type=jnp.float32)


def spectral_table(points, wave_count, row_count):
    lon_ids = jnp.arange(row_count, dtype=jnp.int32)
    col_ids = jnp.arange(2 * wave_count, dtype=jnp.int32)
    wavenumber = jnp.where(col_ids < wave_count, col_ids, col_ids - wave_count + 1)
    phase_index = lon_ids[:, None] * wavenumber[None, :] % points
    angles = 2.0 * math.pi / points * phase_index.astype(jnp.float32)
    trig_value = jnp.where(col_ids[None, :] < wave_count, jnp.cos(angles), jnp.sin(angles))
    col_scale = math.sqrt(2.0 / points) / jnp.sqrt(
        1.0 + 4.0 * wavenumber.astype(jnp.float32) / wave_count
    )
    return trig_value * col_scale[None, :]


def area_weight(start_row, row_count, total_rows):
    row_ids = start_row + jnp.arange(row_count, dtype=jnp.int32)
    colatitude = math.pi * (row_ids.astype(jnp.float32) + 0.5) / (2.0 * total_rows)
    return jnp.sqrt(jnp.sin(colatitude))


def merge_gram(gram_matrix, test_matrix):
    sketch = matmul(gram_matrix, test_matrix)
    sketch_gram = matmul(sketch.T, gram_matrix)
    power_gram = matmul(sketch_gram, sketch)
    power_gram = 0.5 * (power_gram + power_gram.T)
    chol_first = jnp.linalg.cholesky(power_gram)
    projected = lax.linalg.triangular_solve(chol_first, sketch_gram, left_side=True, lower=True)
    proj_gram = matmul(projected, projected.T)
    chol_second = jnp.linalg.cholesky(0.5 * (proj_gram + proj_gram.T))
    unmixed = lax.linalg.triangular_solve(chol_first, sketch.T, left_side=True, lower=True)
    mixing = matmul(chol_second.T, unmixed)
    return (mixing, matmul(chol_second.T, chol_second))


def block_gram(low_energy, cross_term, high_energy):
    top_rows = jnp.concatenate([low_energy, cross_term], axis=1)
    bottom_rows = jnp.concatenate([cross_term.T, high_energy], axis=1)
    return jnp.concatenate([top_rows, bottom_rows], axis=0)


def combine_pair(mixing, low_modes, high_modes):
    rank_rows = low_modes.shape[0]
    return matmul(mixing[:, :rank_rows], low_modes) + matmul(mixing[:, rank_rows:], high_modes)


def own_columns(modes_flat, group_index, group_count):
    col_count = modes_flat.shape[1] // group_count
    return lax.dynamic_slice_in_dim(modes_flat, group_index * col_count, col_count, 1)


def local_tree(snapshots, test_matrix):
    dev_rows = NTH // lax.axis_size("lon")
    dft_table = spectral_table(NPH, MMAX, NPH)
    row_weight = area_weight(lax.axis_index("lon") * dev_rows, dev_rows, NTH)
    spectra = jnp.einsum(
        "pst,pk->stk",
        lax.all_to_all(snapshots, "lon", split_axis=2, concat_axis=0, tiled=True).astype(
            jnp.float32
        ),
        dft_table,
        precision=highest,
    )
    spectra = spectra * row_weight[None, :, None]
    rank_rows = spectra.shape[0]
    modes_now = spectra.reshape(rank_rows, -1)
    levels_count = lax.axis_size("tm").bit_length() - 1
    group_index = lax.axis_index("tm")
    group_count = lax.axis_size("tm")
    energy = lax.psum(matmul(modes_now, modes_now.T), "lon")
    start_level = 0
    for tree_level in range(start_level, levels_count):
        partner_modes, partner_energy = swapped((modes_now, energy), "tm", tree_level)
        is_upper = group_index // 2**tree_level % 2 == 1
        low_modes = jnp.where(is_upper, partner_modes, modes_now)
        high_modes = jnp.where(is_upper, modes_now, partner_modes)
        low_energy = jnp.where(is_upper, partner_energy, energy)
        high_energy = jnp.where(is_upper, energy, partner_energy)
        cross_term = lax.psum(matmul(low_modes, high_modes.T), "lon")
        mixing, energy = merge_gram(block_gram(low_energy, cross_term, high_energy), test_matrix)
        modes_now = combine_pair(mixing, low_modes, high_modes)
    return own_columns(modes_now, group_index, group_count)


def split_table(points, wave_count):
    table = spectral_table(points, wave_count, points // 2)
    table = table.reshape(points // 2, -1, COL_TILE).transpose(1, 0, 2)
    high = lax.reduce_precision(table, 8, 7)
    return jnp.stack([high.astype(jnp.bfloat16), (table - high).astype(jnp.bfloat16)], axis=1)


def ids(shape):
    return lax.broadcasted_iota(jnp.int32, shape, 0), lax.broadcasted_iota(jnp.int32, shape, 1)


def packed_gram(gram):
    rank = gram.shape[0] // 2
    high, cross, low = gram[:rank, :rank], gram[:rank, rank:], gram[rank:, rank:]
    row_ids, col_ids = ids(high.shape)
    both = jnp.where(col_ids >= row_ids, high, low)
    diagonal = jnp.sum(jnp.where(col_ids == row_ids, low, 0.0), axis=0, keepdims=True)
    diagonal = jnp.broadcast_to(jnp.concatenate([diagonal, diagonal], axis=1), (8, 2 * rank))
    return jnp.concatenate([jnp.concatenate([both, cross], axis=1), diagonal], axis=0)


def unpacked_gram(packed):
    rank = packed.shape[1] // 2
    both, cross, diagonal = packed[:rank, :rank], packed[:rank, rank:], packed[rank : rank + 1, :rank]
    row_ids, col_ids = ids(both.shape)
    turned = both.T
    high = jnp.where(col_ids >= row_ids, both, turned)
    low = jnp.where(col_ids < row_ids, both, turned)
    low = jnp.where(col_ids == row_ids, jnp.broadcast_to(diagonal, low.shape), low)
    top = jnp.concatenate([high, cross], axis=1)
    return jnp.concatenate([top, jnp.concatenate([cross.T, low], axis=1)], axis=0)


def relayout_kernel(x_ref, first_ref, last_ref):
    points, some, total = x_ref.shape
    devices, split = first_ref.shape[:2]
    by_snapshot = jnp.transpose(x_ref[...], (1, 0, 2))
    turned = jnp.stack([by_snapshot[i].T for i in range(some)], axis=0)
    rows = jnp.transpose(turned, (1, 0, 2)).reshape(devices, total // devices, some, points)
    first_ref[...] = rows[:, :split]
    last_ref[...] = rows[:, split:]


def relayout(snapshots, devices, split):
    points, rank_rows, total = snapshots.shape
    some = SNAPSHOT_TILE
    cuts = (split, total // devices - split)
    return pl.pallas_call(
        relayout_kernel,
        grid=(rank_rows // some,),
        in_specs=[pl.BlockSpec((points, some, total), lambda i: (0, i, 0))],
        out_specs=[pl.BlockSpec((devices, cut, some, points), lambda i: (0, 0, i, 0)) for cut in cuts],
        out_shape=[
            jax.ShapeDtypeStruct((devices, cut, rank_rows, points), snapshots.dtype) for cut in cuts
        ],
        compiler_params=pltpu.CompilerParams(vmem_limit_bytes=RELAYOUT_VMEM_BYTES),
    )(snapshots)


def spectra_kernel(*refs, first_row):
    weight_ref, x_ref, table_ref, *before, modes_ref, gram_ref, lhs, acc, held, sems, own, own_sems = refs
    sources, groups, rows, rank_rows, points = x_ref.shape
    tiles = table_ref.shape[0]
    span = groups * rank_rows

    def fetch(step):
        return pltpu.make_async_copy(table_ref.at[step], held.at[step], sems.at[step])

    takes = []
    for half in range(2):
        part = pl.ds(half * sources // 2, sources // 2)
        takes.append(pltpu.make_async_copy(x_ref.at[part], own.at[part], own_sems.at[half]))
    for take in takes:
        take.start()
    fetch(0).start()
    acc[...] = jnp.zeros_like(acc)
    for src in range(sources):
        half, place = divmod(src, sources // 2)
        if place == 0:
            takes[half].wait()
            for step in range(1 + half, tiles, 2):
                fetch(step).start()
        for row in range(rows):
            for grp in range(groups):
                start = ((half * rows + row) * groups + grp) * rank_rows
                lhs[start : start + rank_rows, place * points : (place + 1) * points] = own[
                    src, grp, row
                ]

    @pl.loop(0, tiles)
    def _(step):
        fetch(step).wait()
        tile = pl.ds(pl.multiple_of(step * COL_TILE, COL_TILE), COL_TILE)
        values = lhs[...]
        halves = jnp.dot(values, held[step, 0], preferred_element_type=jnp.float32)
        halves += jnp.dot(values, held[step, 1], preferred_element_type=jnp.float32)
        col_ids = step * COL_TILE + lax.broadcasted_iota(jnp.int32, (1, COL_TILE), 1)
        wavenumber = jnp.where(col_ids < MMAX, col_ids, col_ids - MMAX + 1)
        turned = (1 - 2 * (wavenumber & 1)).astype(jnp.float32)
        spectra = halves[: rows * span] + turned * halves[rows * span :]
        tops, rests = [], []
        for row in range(rows):
            scaled = spectra[row * span : (row + 1) * span] * weight_ref[0, first_row + row]
            top = scaled.astype(jnp.bfloat16)
            rest = (scaled - top.astype(jnp.float32)).astype(jnp.bfloat16)
            modes_ref[row, :span, tile] = top
            modes_ref[row, span:, tile] = rest
            tops.append(top)
            rests.append(rest)
        top = jnp.concatenate(tops, axis=1)
        both = jnp.concatenate([top, jnp.concatenate(rests, axis=1)], axis=0)
        acc[...] += lax.dot_general(both, top, NT_DIMS, preferred_element_type=jnp.float32)

    cross = acc[span:, :]
    gram = acc[:span, :] + (cross + cross.T)
    packed = packed_gram(gram)
    for ref in before:
        packed += ref[...]
    gram_ref[...] = packed


def spectra_and_gram(blocks, row_weight, table, first_row, *before):
    sources, groups, rows, rank_rows, points = blocks.shape
    tiles, _, half_lons, _ = table.shape
    cols = tiles * COL_TILE
    span = groups * rank_rows
    packed = (rank_rows + 8, span)
    return pl.pallas_call(
        functools.partial(spectra_kernel, first_row=first_row),
        in_specs=[
            pl.BlockSpec(memory_space=pltpu.SMEM),
            pl.BlockSpec(memory_space=pl.ANY),
            pl.BlockSpec(memory_space=pl.ANY),
            *[pl.BlockSpec(memory_space=pltpu.VMEM) for _ in before],
        ],
        out_specs=[pl.BlockSpec(memory_space=pltpu.VMEM)] * 2,
        out_shape=[
            jax.ShapeDtypeStruct((rows, 2 * span, cols), jnp.bfloat16),
            jax.ShapeDtypeStruct(packed, jnp.float32),
        ],
        scratch_shapes=[
            pltpu.VMEM((2 * rows * span, half_lons), jnp.bfloat16),
            pltpu.VMEM((2 * span, span), jnp.float32),
            pltpu.VMEM(table.shape, table.dtype),
            pltpu.SemaphoreType.DMA((tiles,)),
            pltpu.VMEM(blocks.shape, blocks.dtype),
            pltpu.SemaphoreType.DMA((2,)),
        ],
        compiler_params=pltpu.CompilerParams(vmem_limit_bytes=VMEM_BYTES),
        cost_estimate=pl.CostEstimate(
            flops=8 * rows * span * half_lons * cols,
            bytes_accessed=2 * blocks.size + 4 * half_lons * cols + 4 * rows * span * cols,
            transcendentals=0,
        ),
    )(row_weight.reshape(1, -1), blocks, table, *before)


def dot_full(first, second, dims=(((1,), (0,)), ((), ()))):
    return lax.dot_general(
        first, second, dims, precision=highest, preferred_element_type=jnp.float32
    )


def eliminate(work, size, out_ref):
    height, width = work.shape
    for col in range(0, size, PIVOTS):
        base = col // 8 * 8
        lead = col - base
        rows = [work[lead + i : lead + i + 1, :] for i in range(PIVOTS)]
        cols = [
            jnp.broadcast_to(work[:, col + i : col + i + 1], (height - base, LANES)) for i in range(PIVOTS)
        ]
        update = None
        for i in range(PIVOTS):
            inverse = lax.rsqrt(cols[i][lead + i : lead + i + 1, :])
            wide = jnp.concatenate([inverse] * (width // LANES), axis=1)
            solved = rows[i] * wide
            out_ref[col + i : col + i + 1, :] = solved
            factor = cols[i] * inverse
            for k in range(i + 1, PIVOTS):
                share = factor[lead + k : lead + k + 1, :]
                cols[k] = cols[k] - factor * share
                rows[k] = rows[k] - solved * jnp.concatenate([share] * (width // LANES), axis=1)
            term = jnp.concatenate([factor] * (width // LANES), axis=1) * solved
            update = term if update is None else update + term
        following = (col + PIVOTS) // 8 * 8 - base
        work = work[following:] - update[following:]


def add_up(parts):
    while len(parts) > 1:
        parts = [parts[i] + parts[i + 1] for i in range(0, len(parts), 2)]
    return parts[0]


def merge_kernel(*refs, split):
    *part_refs, test_ref, early_ref, late_ref, out_ref, mix_ref, first_ref, second_ref, held, sems = refs
    rank = test_ref.shape[0]
    row = pl.program_id(0)
    fetches = [
        pltpu.make_async_copy(early_ref, held.at[pl.ds(0, split)], sems.at[0]),
        pltpu.make_async_copy(late_ref, held.at[pl.ds(split, late_ref.shape[0])], sems.at[1]),
    ]

    @pl.when(row == 0)
    def _():
        for fetch in fetches:
            fetch.start()
        gram = unpacked_gram(add_up([part[...] for part in part_refs]))
        test_t = test_ref[...]
        sketch = dot_full(gram, test_t, NT_DIMS)
        sketch_t = dot_full(test_t, gram)
        sketch_gram = dot_full(sketch_t, gram)
        power = dot_full(sketch_gram, sketch)
        power = 0.5 * (power + power.T)
        pad = jnp.zeros_like(power)
        eliminate(jnp.concatenate([power, pad, sketch_gram, sketch_t], axis=1), rank, first_ref)
        projected = first_ref[:, 2 * rank : 4 * rank]
        unmixed = first_ref[:, 4 * rank : 6 * rank]
        inner = dot_full(projected, projected, NT_DIMS)
        inner = 0.5 * (inner + inner.T)
        eliminate(jnp.concatenate([inner, pad], axis=1), rank, second_ref)
        upper = second_ref[:, :rank]
        row_ids, col_ids = ids(upper.shape)
        mixing = dot_full(jnp.where(col_ids >= row_ids, upper, 0.0), unmixed)
        top = mixing.astype(jnp.bfloat16)
        rest = (mixing - top.astype(jnp.float32)).astype(jnp.bfloat16)
        mix_ref[:rank, : 2 * rank] = top
        mix_ref[:rank, 2 * rank :] = top
        mix_ref[rank:, : 2 * rank] = rest
        mix_ref[rank:, 2 * rank :] = jnp.zeros_like(rest)

        for fetch in fetches:
            fetch.wait()

    cols = held.shape[2]
    for i in range(out_ref.shape[1] // cols):
        modes = held[row * (out_ref.shape[1] // cols) + i]
        both = jnp.dot(mix_ref[...], modes, preferred_element_type=jnp.float32)
        out_ref[:, i * cols : (i + 1) * cols] = both[:rank] + both[rank:]


def merge_and_mix(gram_parts, test_matrix, early, late):
    split, height, cols = early.shape
    rows = split + late.shape[0]
    some = rows if rows % 2 else rows // 2
    rank = test_matrix.shape[1]
    return pl.pallas_call(
        functools.partial(merge_kernel, split=split),
        grid=(rows // some,),
        in_specs=[
            *[pl.BlockSpec(part.shape, lambda i: (0, 0)) for part in gram_parts],
            pl.BlockSpec((rank, 2 * rank), lambda i: (0, 0)),
            pl.BlockSpec(memory_space=pl.ANY),
            pl.BlockSpec(memory_space=pl.ANY),
        ],
        out_specs=pl.BlockSpec((rank, some * cols), lambda i: (0, i)),
        out_shape=jax.ShapeDtypeStruct((rank, rows * cols), jnp.float32),
        scratch_shapes=[
            pltpu.VMEM((2 * rank, height), jnp.bfloat16),
            pltpu.VMEM((rank, 6 * rank), jnp.float32),
            pltpu.VMEM((rank, 2 * rank), jnp.float32),
            pltpu.VMEM((rows, height, cols), jnp.bfloat16),
            pltpu.SemaphoreType.DMA((2,)),
        ],
        compiler_params=pltpu.CompilerParams(vmem_limit_bytes=VMEM_BYTES),
    )(*gram_parts, test_matrix.T, early, late)


def exchanged(array, axes, bits):
    count = lax.axis_size(axes)
    masks = [0]
    for bit in bits:
        masks += [mask | bit for mask in masks]
    return [array] + [
        lax.ppermute(array, axes, [(i, i ^ mask) for i in range(count)]) for mask in masks[1:]
    ]


def sum_parts(array, axes):
    bits = [1 << k for k in range(lax.axis_size(axes).bit_length() - 1)]
    parts = exchanged(array, axes, bits[:1])
    for group in (bits[1:2] + bits[-1:], *[bits[k : k + 2] for k in range(2, len(bits) - 1, 2)]):
        parts = exchanged(add_up(parts), axes, group)
    return parts


def local_pair(snapshots, test_matrix):
    points, rank_rows, total_rows = snapshots.shape
    lon_count, group_count = lax.axis_size("lon"), lax.axis_size("tm")
    dev_rows = total_rows // (lon_count * group_count)
    first_row = (lax.axis_index("lon") * group_count + lax.axis_index("tm")) * dev_rows
    row_weight = area_weight(first_row, dev_rows, NTH)
    table = split_table(NPH, MMAX)
    split = EARLY_ROWS * dev_rows // 8
    early, late = relayout(snapshots, lon_count * group_count, split)
    late, table = lax.optimization_barrier((late, table))
    modes, gram = [], []
    for first, part in ((0, early), (split, late)):
        blocks = lax.all_to_all(part, ("lon", "tm"), split_axis=0, concat_axis=0, tiled=True)
        blocks = blocks.reshape(lon_count, group_count, -1, rank_rows, points)
        spectra, *gram = spectra_and_gram(blocks, row_weight, table, first, *gram)
        modes.append(spectra)
    return merge_and_mix(sum_parts(gram[0], ("tm", "lon")), test_matrix, *modes)


def solution(mesh):
    lon_count, group_count = mesh.shape["lon"], mesh.shape["tm"]
    device_count = lon_count * group_count
    whole_rows = NTH % device_count == 0 and NTH >= 2 * device_count
    whole_rows = whole_rows and device_count & (device_count - 1) == 0
    return jax.shard_map(
        local_pair if group_count == 2 and whole_rows else local_tree,
        mesh=mesh,
        in_specs=(P("lon", "tm", None), P()),
        out_specs=P(None, ("lon", "tm")),
        check_vma=False,
    )
```

```python
import functools
import math

import jax
import jax.numpy as jnp
from jax import lax
from jax.experimental import pallas as pl
from jax.experimental.pallas import tpu as pltpu
from jax.sharding import PartitionSpec as P

NPH = 2048
MMAX = 640
NTH = 256
COL_TILE = 256
LANES = 128
PIVOTS = 16
SNAPSHOT_TILE = 16
EARLY_ROWS = 6
VMEM_BYTES = 50 * 2**20
RELAYOUT_VMEM_BYTES = 58 * 2**20


highest = lax.Precision.HIGHEST
NT_DIMS = (((1,), (1,)), ((), ()))


def swapped(array, axis, distance):
    return lax.ppermute(array, axis, [(i, i ^ 1 << distance) for i in range(lax.axis_size(axis))])


def matmul(first_op, second_op):
    return jnp.dot(first_op, second_op, precision=highest, preferred_element_type=jnp.float32)


def spectral_table(points, wave_count, row_count):
    lon_ids = jnp.arange(row_count, dtype=jnp.int32)
    col_ids = jnp.arange(2 * wave_count, dtype=jnp.int32)
    wavenumber = jnp.where(col_ids < wave_count, col_ids, col_ids - wave_count + 1)
    phase_index = lon_ids[:, None] * wavenumber[None, :] % points
    angles = 2.0 * math.pi / points * phase_index.astype(jnp.float32)
    trig_value = jnp.where(col_ids[None, :] < wave_count, jnp.cos(angles), jnp.sin(angles))
    col_scale = math.sqrt(2.0 / points) / jnp.sqrt(
        1.0 + 4.0 * wavenumber.astype(jnp.float32) / wave_count
    )
    return trig_value * col_scale[None, :]


def area_weight(start_row, row_count, total_rows):
    row_ids = start_row + jnp.arange(row_count, dtype=jnp.int32)
    colatitude = math.pi * (row_ids.astype(jnp.float32) + 0.5) / (2.0 * total_rows)
    return jnp.sqrt(jnp.sin(colatitude))


def merge_gram(gram_matrix, test_matrix):
    sketch = matmul(gram_matrix, test_matrix)
    sketch_gram = matmul(sketch.T, gram_matrix)
    power_gram = matmul(sketch_gram, sketch)
    power_gram = 0.5 * (power_gram + power_gram.T)
    chol_first = jnp.linalg.cholesky(power_gram)
    projected = lax.linalg.triangular_solve(chol_first, sketch_gram, left_side=True, lower=True)
    proj_gram = matmul(projected, projected.T)
    chol_second = jnp.linalg.cholesky(0.5 * (proj_gram + proj_gram.T))
    unmixed = lax.linalg.triangular_solve(chol_first, sketch.T, left_side=True, lower=True)
    mixing = matmul(chol_second.T, unmixed)
    return (mixing, matmul(chol_second.T, chol_second))


def block_gram(low_energy, cross_term, high_energy):
    top_rows = jnp.concatenate([low_energy, cross_term], axis=1)
    bottom_rows = jnp.concatenate([cross_term.T, high_energy], axis=1)
    return jnp.concatenate([top_rows, bottom_rows], axis=0)


def combine_pair(mixing, low_modes, high_modes):
    rank_rows = low_modes.shape[0]
    return matmul(mixing[:, :rank_rows], low_modes) + matmul(mixing[:, rank_rows:], high_modes)


def own_columns(modes_flat, group_index, group_count):
    col_count = modes_flat.shape[1] // group_count
    return lax.dynamic_slice_in_dim(modes_flat, group_index * col_count, col_count, 1)


def local_tree(snapshots, test_matrix):
    dev_rows = NTH // lax.axis_size("lon")
    dft_table = spectral_table(NPH, MMAX, NPH)
    row_weight = area_weight(lax.axis_index("lon") * dev_rows, dev_rows, NTH)
    spectra = jnp.einsum(
        "pst,pk->stk",
        lax.all_to_all(snapshots, "lon", split_axis=2, concat_axis=0, tiled=True).astype(
            jnp.float32
        ),
        dft_table,
        precision=highest,
    )
    spectra = spectra * row_weight[None, :, None]
    rank_rows = spectra.shape[0]
    modes_now = spectra.reshape(rank_rows, -1)
    levels_count = lax.axis_size("tm").bit_length() - 1
    group_index = lax.axis_index("tm")
    group_count = lax.axis_size("tm")
    energy = lax.psum(matmul(modes_now, modes_now.T), "lon")
    start_level = 0
    for tree_level in range(start_level, levels_count):
        partner_modes, partner_energy = swapped((modes_now, energy), "tm", tree_level)
        is_upper = group_index // 2**tree_level % 2 == 1
        low_modes = jnp.where(is_upper, partner_modes, modes_now)
        high_modes = jnp.where(is_upper, modes_now, partner_modes)
        low_energy = jnp.where(is_upper, partner_energy, energy)
        high_energy = jnp.where(is_upper, energy, partner_energy)
        cross_term = lax.psum(matmul(low_modes, high_modes.T), "lon")
        mixing, energy = merge_gram(block_gram(low_energy, cross_term, high_energy), test_matrix)
        modes_now = combine_pair(mixing, low_modes, high_modes)
    return own_columns(modes_now, group_index, group_count)


def split_table(points, wave_count):
    table = spectral_table(points, wave_count, points // 2)
    table = table.reshape(points // 2, -1, COL_TILE).transpose(1, 0, 2)
    high = lax.reduce_precision(table, 8, 7)
    return jnp.stack([high.astype(jnp.bfloat16), (table - high).astype(jnp.bfloat16)], axis=1)


def ids(shape):
    return lax.broadcasted_iota(jnp.int32, shape, 0), lax.broadcasted_iota(jnp.int32, shape, 1)


def packed_gram(gram):
    rank = gram.shape[0] // 2
    high, cross, low = gram[:rank, :rank], gram[:rank, rank:], gram[rank:, rank:]
    row_ids, col_ids = ids(high.shape)
    both = jnp.where(col_ids >= row_ids, high, low)
    diagonal = jnp.sum(jnp.where(col_ids == row_ids, low, 0.0), axis=0, keepdims=True)
    diagonal = jnp.broadcast_to(jnp.concatenate([diagonal, diagonal], axis=1), (8, 2 * rank))
    return jnp.concatenate([jnp.concatenate([both, cross], axis=1), diagonal], axis=0)


def unpacked_gram(packed):
    rank = packed.shape[1] // 2
    both, cross, diagonal = packed[:rank, :rank], packed[:rank, rank:], packed[rank : rank + 1, :rank]
    row_ids, col_ids = ids(both.shape)
    turned = both.T
    high = jnp.where(col_ids >= row_ids, both, turned)
    low = jnp.where(col_ids < row_ids, both, turned)
    low = jnp.where(col_ids == row_ids, jnp.broadcast_to(diagonal, low.shape), low)
    top = jnp.concatenate([high, cross], axis=1)
    return jnp.concatenate([top, jnp.concatenate([cross.T, low], axis=1)], axis=0)


def relayout_kernel(x_ref, first_ref, last_ref):
    points, some, total = x_ref.shape
    devices, split = first_ref.shape[:2]
    by_snapshot = jnp.transpose(x_ref[...], (1, 0, 2))
    turned = jnp.stack([by_snapshot[i].T for i in range(some)], axis=0)
    rows = jnp.transpose(turned, (1, 0, 2)).reshape(devices, total // devices, some, points)
    first_ref[...] = rows[:, :split]
    last_ref[...] = rows[:, split:]


def relayout(snapshots, devices, split):
    points, rank_rows, total = snapshots.shape
    some = SNAPSHOT_TILE
    cuts = (split, total // devices - split)
    return pl.pallas_call(
        relayout_kernel,
        grid=(rank_rows // some,),
        in_specs=[pl.BlockSpec((points, some, total), lambda i: (0, i, 0))],
        out_specs=[pl.BlockSpec((devices, cut, some, points), lambda i: (0, 0, i, 0)) for cut in cuts],
        out_shape=[
            jax.ShapeDtypeStruct((devices, cut, rank_rows, points), snapshots.dtype) for cut in cuts
        ],
        compiler_params=pltpu.CompilerParams(vmem_limit_bytes=RELAYOUT_VMEM_BYTES),
    )(snapshots)


def spectra_kernel(*refs, first_row):
    weight_ref, x_ref, table_ref, *before, modes_ref, gram_ref, lhs, held, sems, own, own_sems = refs
    sources, groups, rows, rank_rows, points = x_ref.shape
    tiles = table_ref.shape[0]
    span = groups * rank_rows

    def fetch(step):
        return pltpu.make_async_copy(table_ref.at[step], held.at[step], sems.at[step])

    takes = []
    for half in range(2):
        part = pl.ds(half * sources // 2, sources // 2)
        takes.append(pltpu.make_async_copy(x_ref.at[part], own.at[part], own_sems.at[half]))
    for take in takes:
        take.start()
    fetch(0).start()
    for src in range(sources):
        half, place = divmod(src, sources // 2)
        if place == 0:
            takes[half].wait()
            for step in range(1 + half, tiles, 2):
                fetch(step).start()
        for row in range(rows):
            for grp in range(groups):
                start = ((half * rows + row) * groups + grp) * rank_rows
                lhs[start : start + rank_rows, place * points : (place + 1) * points] = own[
                    src, grp, row
                ]

    @pl.loop(0, tiles)
    def _(step):
        fetch(step).wait()
        tile = pl.ds(pl.multiple_of(step * COL_TILE, COL_TILE), COL_TILE)
        values = lhs[...]
        halves = jnp.dot(values, held[step, 0], preferred_element_type=jnp.float32)
        halves += jnp.dot(values, held[step, 1], preferred_element_type=jnp.float32)
        col_ids = step * COL_TILE + lax.broadcasted_iota(jnp.int32, (1, COL_TILE), 1)
        wavenumber = jnp.where(col_ids < MMAX, col_ids, col_ids - MMAX + 1)
        turned = (1 - 2 * (wavenumber & 1)).astype(jnp.float32)
        spectra = halves[: rows * span] + turned * halves[rows * span :]
        for row in range(rows):
            scaled = spectra[row * span : (row + 1) * span] * weight_ref[0, first_row + row]
            top = scaled.astype(jnp.bfloat16)
            rest = (scaled - top.astype(jnp.float32)).astype(jnp.bfloat16)
            modes_ref[row, :span, tile] = top
            modes_ref[row, span:, tile] = rest

    products = [
        lax.dot_general(
            modes_ref[row], modes_ref[row, :span, :], NT_DIMS, preferred_element_type=jnp.float32
        )
        for row in range(rows)
    ]
    total = functools.reduce(jnp.add, products)
    cross = total[span:]
    gram = total[:span] + (cross + cross.T)
    packed = packed_gram(gram)
    for ref in before:
        packed += ref[...]
    gram_ref[...] = packed


def spectra_and_gram(blocks, row_weight, table, first_row, *before):
    sources, groups, rows, rank_rows, points = blocks.shape
    tiles, _, half_lons, _ = table.shape
    cols = tiles * COL_TILE
    span = groups * rank_rows
    packed = (rank_rows + 8, span)
    return pl.pallas_call(
        functools.partial(spectra_kernel, first_row=first_row),
        in_specs=[
            pl.BlockSpec(memory_space=pltpu.SMEM),
            pl.BlockSpec(memory_space=pl.ANY),
            pl.BlockSpec(memory_space=pl.ANY),
            *[pl.BlockSpec(memory_space=pltpu.VMEM) for _ in before],
        ],
        out_specs=[pl.BlockSpec(memory_space=pltpu.VMEM)] * 2,
        out_shape=[
            jax.ShapeDtypeStruct((rows, 2 * span, cols), jnp.bfloat16),
            jax.ShapeDtypeStruct(packed, jnp.float32),
        ],
        scratch_shapes=[
            pltpu.VMEM((2 * rows * span, half_lons), jnp.bfloat16),
            pltpu.VMEM(table.shape, table.dtype),
            pltpu.SemaphoreType.DMA((tiles,)),
            pltpu.VMEM(blocks.shape, blocks.dtype),
            pltpu.SemaphoreType.DMA((2,)),
        ],
        compiler_params=pltpu.CompilerParams(vmem_limit_bytes=VMEM_BYTES),
        cost_estimate=pl.CostEstimate(
            flops=8 * rows * span * half_lons * cols,
            bytes_accessed=2 * blocks.size + 4 * half_lons * cols + 4 * rows * span * cols,
            transcendentals=0,
        ),
    )(row_weight.reshape(1, -1), blocks, table, *before)


def dot_full(first, second, dims=(((1,), (0,)), ((), ()))):
    return lax.dot_general(
        first, second, dims, precision=highest, preferred_element_type=jnp.float32
    )


def eliminate(work, size, out_ref):
    height, width = work.shape
    for col in range(0, size, PIVOTS):
        base = col // 8 * 8
        lead = col - base
        rows = [work[lead + i : lead + i + 1, :] for i in range(PIVOTS)]
        cols = [
            jnp.broadcast_to(work[:, col + i : col + i + 1], (height - base, LANES)) for i in range(PIVOTS)
        ]
        update = None
        for i in range(PIVOTS):
            inverse = lax.rsqrt(cols[i][lead + i : lead + i + 1, :])
            wide = jnp.concatenate([inverse] * (width // LANES), axis=1)
            solved = rows[i] * wide
            out_ref[col + i : col + i + 1, :] = solved
            factor = cols[i] * inverse
            for k in range(i + 1, PIVOTS):
                share = factor[lead + k : lead + k + 1, :]
                cols[k] = cols[k] - factor * share
                rows[k] = rows[k] - solved * jnp.concatenate([share] * (width // LANES), axis=1)
            term = jnp.concatenate([factor] * (width // LANES), axis=1) * solved
            update = term if update is None else update + term
        following = (col + PIVOTS) // 8 * 8 - base
        work = work[following:] - update[following:]


def add_up(parts):
    while len(parts) > 1:
        parts = [parts[i] + parts[i + 1] for i in range(0, len(parts), 2)]
    return parts[0]


def merge_kernel(*refs, split):
    *part_refs, test_ref, early_ref, late_ref, out_ref, mix_ref, first_ref, second_ref, held, sems = refs
    rank = test_ref.shape[0]
    row = pl.program_id(0)
    fetches = [
        pltpu.make_async_copy(early_ref, held.at[pl.ds(0, split)], sems.at[0]),
        pltpu.make_async_copy(late_ref, held.at[pl.ds(split, late_ref.shape[0])], sems.at[1]),
    ]

    @pl.when(row == 0)
    def _():
        for fetch in fetches:
            fetch.start()
        gram = unpacked_gram(add_up([part[...] for part in part_refs]))
        test_t = test_ref[...]
        sketch = dot_full(gram, test_t, NT_DIMS)
        sketch_t = dot_full(test_t, gram)
        sketch_gram = dot_full(sketch_t, gram)
        power = dot_full(sketch_gram, sketch)
        power = 0.5 * (power + power.T)
        pad = jnp.zeros_like(power)
        eliminate(jnp.concatenate([power, pad, sketch_gram, sketch_t], axis=1), rank, first_ref)
        projected = first_ref[:, 2 * rank : 4 * rank]
        unmixed = first_ref[:, 4 * rank : 6 * rank]
        inner = dot_full(projected, projected, NT_DIMS)
        inner = 0.5 * (inner + inner.T)
        eliminate(jnp.concatenate([inner, pad], axis=1), rank, second_ref)
        upper = second_ref[:, :rank]
        row_ids, col_ids = ids(upper.shape)
        mixing = dot_full(jnp.where(col_ids >= row_ids, upper, 0.0), unmixed)
        top = mixing.astype(jnp.bfloat16)
        rest = (mixing - top.astype(jnp.float32)).astype(jnp.bfloat16)
        mix_ref[:rank, : 2 * rank] = top
        mix_ref[:rank, 2 * rank :] = top
        mix_ref[rank:, : 2 * rank] = rest
        mix_ref[rank:, 2 * rank :] = jnp.zeros_like(rest)

        for fetch in fetches:
            fetch.wait()

    cols = held.shape[2]
    for i in range(out_ref.shape[1] // cols):
        modes = held[row * (out_ref.shape[1] // cols) + i]
        both = jnp.dot(mix_ref[...], modes, preferred_element_type=jnp.float32)
        out_ref[:, i * cols : (i + 1) * cols] = both[:rank] + both[rank:]


def merge_and_mix(gram_parts, test_matrix, early, late):
    split, height, cols = early.shape
    rows = split + late.shape[0]
    some = rows if rows % 2 else rows // 2
    rank = test_matrix.shape[1]
    return pl.pallas_call(
        functools.partial(merge_kernel, split=split),
        grid=(rows // some,),
        in_specs=[
            *[pl.BlockSpec(part.shape, lambda i: (0, 0)) for part in gram_parts],
            pl.BlockSpec((rank, 2 * rank), lambda i: (0, 0)),
            pl.BlockSpec(memory_space=pl.ANY),
            pl.BlockSpec(memory_space=pl.ANY),
        ],
        out_specs=pl.BlockSpec((rank, some * cols), lambda i: (0, i)),
        out_shape=jax.ShapeDtypeStruct((rank, rows * cols), jnp.float32),
        scratch_shapes=[
            pltpu.VMEM((2 * rank, height), jnp.bfloat16),
            pltpu.VMEM((rank, 6 * rank), jnp.float32),
            pltpu.VMEM((rank, 2 * rank), jnp.float32),
            pltpu.VMEM((rows, height, cols), jnp.bfloat16),
            pltpu.SemaphoreType.DMA((2,)),
        ],
        compiler_params=pltpu.CompilerParams(vmem_limit_bytes=VMEM_BYTES),
    )(*gram_parts, test_matrix.T, early, late)


def exchanged(array, axes, bits):
    count = lax.axis_size(axes)
    masks = [0]
    for bit in bits:
        masks += [mask | bit for mask in masks]
    return [array] + [
        lax.ppermute(array, axes, [(i, i ^ mask) for i in range(count)]) for mask in masks[1:]
    ]


def sum_parts(array, axes):
    bits = [1 << k for k in range(lax.axis_size(axes).bit_length() - 1)]
    parts = exchanged(array, axes, bits[:1])
    for group in (bits[1:2] + bits[-1:], *[bits[k : k + 2] for k in range(2, len(bits) - 1, 2)]):
        parts = exchanged(add_up(parts), axes, group)
    return parts


def local_pair(snapshots, test_matrix):
    points, rank_rows, total_rows = snapshots.shape
    lon_count, group_count = lax.axis_size("lon"), lax.axis_size("tm")
    dev_rows = total_rows // (lon_count * group_count)
    first_row = (lax.axis_index("lon") * group_count + lax.axis_index("tm")) * dev_rows
    row_weight = area_weight(first_row, dev_rows, NTH)
    table = split_table(NPH, MMAX)
    split = EARLY_ROWS * dev_rows // 8
    early, late = relayout(snapshots, lon_count * group_count, split)
    late, table = lax.optimization_barrier((late, table))
    modes, gram = [], []
    for first, part in ((0, early), (split, late)):
        blocks = lax.all_to_all(part, ("lon", "tm"), split_axis=0, concat_axis=0, tiled=True)
        blocks = blocks.reshape(lon_count, group_count, -1, rank_rows, points)
        spectra, *gram = spectra_and_gram(blocks, row_weight, table, first, *gram)
        modes.append(spectra)
    return merge_and_mix(sum_parts(gram[0], ("tm", "lon")), test_matrix, *modes)


def solution(mesh):
    lon_count, group_count = mesh.shape["lon"], mesh.shape["tm"]
    device_count = lon_count * group_count
    whole_rows = NTH % device_count == 0 and NTH >= 2 * device_count
    whole_rows = whole_rows and device_count & (device_count - 1) == 0
    return jax.shard_map(
        local_pair if group_count == 2 and whole_rows else local_tree,
        mesh=mesh,
        in_specs=(P("lon", "tm", None), P()),
        out_specs=P(None, ("lon", "tm")),
        check_vma=False,
    )
```

```python
import functools
import math

import jax
import jax.numpy as jnp
from jax import lax
from jax.experimental import pallas as pl
from jax.experimental.pallas import tpu as pltpu
from jax.sharding import PartitionSpec as P

NPH = 2048
MMAX = 640
NTH = 256
COL_TILE = 256
LANES = 128
PIVOTS = 16
SNAPSHOT_TILE = 32
EARLY_ROWS = 6
VMEM_BYTES = 50 * 2**20
RELAYOUT_VMEM_BYTES = 58 * 2**20


highest = lax.Precision.HIGHEST
NT_DIMS = (((1,), (1,)), ((), ()))


def swapped(array, axis, distance):
    return lax.ppermute(array, axis, [(i, i ^ 1 << distance) for i in range(lax.axis_size(axis))])


def matmul(first_op, second_op):
    return jnp.dot(first_op, second_op, precision=highest, preferred_element_type=jnp.float32)


def spectral_table(points, wave_count, row_count):
    lon_ids = jnp.arange(row_count, dtype=jnp.int32)
    col_ids = jnp.arange(2 * wave_count, dtype=jnp.int32)
    wavenumber = jnp.where(col_ids < wave_count, col_ids, col_ids - wave_count + 1)
    phase_index = lon_ids[:, None] * wavenumber[None, :] % points
    angles = 2.0 * math.pi / points * phase_index.astype(jnp.float32)
    trig_value = jnp.where(col_ids[None, :] < wave_count, jnp.cos(angles), jnp.sin(angles))
    col_scale = math.sqrt(2.0 / points) / jnp.sqrt(
        1.0 + 4.0 * wavenumber.astype(jnp.float32) / wave_count
    )
    return trig_value * col_scale[None, :]


def area_weight(start_row, row_count, total_rows):
    row_ids = start_row + jnp.arange(row_count, dtype=jnp.int32)
    colatitude = math.pi * (row_ids.astype(jnp.float32) + 0.5) / (2.0 * total_rows)
    return jnp.sqrt(jnp.sin(colatitude))


def merge_gram(gram_matrix, test_matrix):
    sketch = matmul(gram_matrix, test_matrix)
    sketch_gram = matmul(sketch.T, gram_matrix)
    power_gram = matmul(sketch_gram, sketch)
    power_gram = 0.5 * (power_gram + power_gram.T)
    chol_first = jnp.linalg.cholesky(power_gram)
    projected = lax.linalg.triangular_solve(chol_first, sketch_gram, left_side=True, lower=True)
    proj_gram = matmul(projected, projected.T)
    chol_second = jnp.linalg.cholesky(0.5 * (proj_gram + proj_gram.T))
    unmixed = lax.linalg.triangular_solve(chol_first, sketch.T, left_side=True, lower=True)
    mixing = matmul(chol_second.T, unmixed)
    return (mixing, matmul(chol_second.T, chol_second))


def block_gram(low_energy, cross_term, high_energy):
    top_rows = jnp.concatenate([low_energy, cross_term], axis=1)
    bottom_rows = jnp.concatenate([cross_term.T, high_energy], axis=1)
    return jnp.concatenate([top_rows, bottom_rows], axis=0)


def combine_pair(mixing, low_modes, high_modes):
    rank_rows = low_modes.shape[0]
    return matmul(mixing[:, :rank_rows], low_modes) + matmul(mixing[:, rank_rows:], high_modes)


def own_columns(modes_flat, group_index, group_count):
    col_count = modes_flat.shape[1] // group_count
    return lax.dynamic_slice_in_dim(modes_flat, group_index * col_count, col_count, 1)


def local_tree(snapshots, test_matrix):
    dev_rows = NTH // lax.axis_size("lon")
    dft_table = spectral_table(NPH, MMAX, NPH)
    row_weight = area_weight(lax.axis_index("lon") * dev_rows, dev_rows, NTH)
    spectra = jnp.einsum(
        "pst,pk->stk",
        lax.all_to_all(snapshots, "lon", split_axis=2, concat_axis=0, tiled=True).astype(
            jnp.float32
        ),
        dft_table,
        precision=highest,
    )
    spectra = spectra * row_weight[None, :, None]
    rank_rows = spectra.shape[0]
    modes_now = spectra.reshape(rank_rows, -1)
    levels_count = lax.axis_size("tm").bit_length() - 1
    group_index = lax.axis_index("tm")
    group_count = lax.axis_size("tm")
    energy = lax.psum(matmul(modes_now, modes_now.T), "lon")
    start_level = 0
    for tree_level in range(start_level, levels_count):
        partner_modes, partner_energy = swapped((modes_now, energy), "tm", tree_level)
        is_upper = group_index // 2**tree_level % 2 == 1
        low_modes = jnp.where(is_upper, partner_modes, modes_now)
        high_modes = jnp.where(is_upper, modes_now, partner_modes)
        low_energy = jnp.where(is_upper, partner_energy, energy)
        high_energy = jnp.where(is_upper, energy, partner_energy)
        cross_term = lax.psum(matmul(low_modes, high_modes.T), "lon")
        mixing, energy = merge_gram(block_gram(low_energy, cross_term, high_energy), test_matrix)
        modes_now = combine_pair(mixing, low_modes, high_modes)
    return own_columns(modes_now, group_index, group_count)


def split_table(points, wave_count):
    table = spectral_table(points, wave_count, points // 2)
    table = table.reshape(points // 2, -1, COL_TILE).transpose(1, 0, 2)
    high = lax.reduce_precision(table, 8, 7)
    return jnp.stack([high.astype(jnp.bfloat16), (table - high).astype(jnp.bfloat16)], axis=1)


def ids(shape):
    return lax.broadcasted_iota(jnp.int32, shape, 0), lax.broadcasted_iota(jnp.int32, shape, 1)


def packed_gram(gram):
    rank = gram.shape[0] // 2
    high, cross, low = gram[:rank, :rank], gram[:rank, rank:], gram[rank:, rank:]
    row_ids, col_ids = ids(high.shape)
    both = jnp.where(col_ids >= row_ids, high, low)
    diagonal = jnp.sum(jnp.where(col_ids == row_ids, low, 0.0), axis=0, keepdims=True)
    diagonal = jnp.broadcast_to(jnp.concatenate([diagonal, diagonal], axis=1), (8, 2 * rank))
    return jnp.concatenate([jnp.concatenate([both, cross], axis=1), diagonal], axis=0)


def unpacked_gram(packed):
    rank = packed.shape[1] // 2
    both, cross, diagonal = packed[:rank, :rank], packed[:rank, rank:], packed[rank : rank + 1, :rank]
    row_ids, col_ids = ids(both.shape)
    turned = both.T
    high = jnp.where(col_ids >= row_ids, both, turned)
    low = jnp.where(col_ids < row_ids, both, turned)
    low = jnp.where(col_ids == row_ids, jnp.broadcast_to(diagonal, low.shape), low)
    top = jnp.concatenate([high, cross], axis=1)
    return jnp.concatenate([top, jnp.concatenate([cross.T, low], axis=1)], axis=0)


def relayout_kernel(x_ref, first_ref, last_ref):
    points, some, total = x_ref.shape
    devices, split = first_ref.shape[:2]
    by_snapshot = jnp.transpose(x_ref[...], (1, 0, 2))
    turned = jnp.stack([by_snapshot[i].T for i in range(some)], axis=0)
    rows = jnp.transpose(turned, (1, 0, 2)).reshape(devices, total // devices, some, points)
    first_ref[...] = rows[:, :split]
    last_ref[...] = rows[:, split:]


def relayout(snapshots, devices, split):
    points, rank_rows, total = snapshots.shape
    some = SNAPSHOT_TILE
    cuts = (split, total // devices - split)
    return pl.pallas_call(
        relayout_kernel,
        grid=(rank_rows // some,),
        in_specs=[pl.BlockSpec((points, some, total), lambda i: (0, i, 0))],
        out_specs=[pl.BlockSpec((devices, cut, some, points), lambda i: (0, 0, i, 0)) for cut in cuts],
        out_shape=[
            jax.ShapeDtypeStruct((devices, cut, rank_rows, points), snapshots.dtype) for cut in cuts
        ],
        compiler_params=pltpu.CompilerParams(vmem_limit_bytes=RELAYOUT_VMEM_BYTES),
    )(snapshots)


def spectra_kernel(*refs, first_row):
    weight_ref, x_ref, table_ref, *before, modes_ref, gram_ref, lhs, held, sems, own, own_sems = refs
    sources, groups, rows, rank_rows, points = x_ref.shape
    tiles = table_ref.shape[0]
    span = groups * rank_rows

    def fetch(step):
        return pltpu.make_async_copy(table_ref.at[step], held.at[step], sems.at[step])

    takes = []
    for half in range(2):
        part = pl.ds(half * sources // 2, sources // 2)
        takes.append(pltpu.make_async_copy(x_ref.at[part], own.at[part], own_sems.at[half]))
    for take in takes:
        take.start()
    fetch(0).start()
    for src in range(sources):
        half, place = divmod(src, sources // 2)
        if place == 0:
            takes[half].wait()
            for step in range(1 + half, tiles, 2):
                fetch(step).start()
        for row in range(rows):
            for grp in range(groups):
                start = ((half * rows + row) * groups + grp) * rank_rows
                lhs[start : start + rank_rows, place * points : (place + 1) * points] = own[
                    src, grp, row
                ]

    @pl.loop(0, tiles)
    def _(step):
        fetch(step).wait()
        tile = pl.ds(pl.multiple_of(step * COL_TILE, COL_TILE), COL_TILE)
        values = lhs[...]
        halves = jnp.dot(values, held[step, 0], preferred_element_type=jnp.float32)
        halves += jnp.dot(values, held[step, 1], preferred_element_type=jnp.float32)
        col_ids = step * COL_TILE + lax.broadcasted_iota(jnp.int32, (1, COL_TILE), 1)
        wavenumber = jnp.where(col_ids < MMAX, col_ids, col_ids - MMAX + 1)
        turned = (1 - 2 * (wavenumber & 1)).astype(jnp.float32)
        spectra = halves[: rows * span] + turned * halves[rows * span :]
        for row in range(rows):
            scaled = spectra[row * span : (row + 1) * span] * weight_ref[0, first_row + row]
            top = scaled.astype(jnp.bfloat16)
            rest = (scaled - top.astype(jnp.float32)).astype(jnp.bfloat16)
            modes_ref[row, :span, tile] = top
            modes_ref[row, span:, tile] = rest

    products = [
        lax.dot_general(
            modes_ref[row], modes_ref[row, :span, :], NT_DIMS, preferred_element_type=jnp.float32
        )
        for row in range(rows)
    ]
    total = functools.reduce(jnp.add, products)
    cross = total[span:]
    gram = total[:span] + (cross + cross.T)
    packed = packed_gram(gram)
    for ref in before:
        packed += ref[...]
    gram_ref[...] = packed


def spectra_and_gram(blocks, row_weight, table, first_row, *before):
    sources, groups, rows, rank_rows, points = blocks.shape
    tiles, _, half_lons, _ = table.shape
    cols = tiles * COL_TILE
    span = groups * rank_rows
    packed = (rank_rows + 8, span)
    return pl.pallas_call(
        functools.partial(spectra_kernel, first_row=first_row),
        in_specs=[
            pl.BlockSpec(memory_space=pltpu.SMEM),
            pl.BlockSpec(memory_space=pl.ANY),
            pl.BlockSpec(memory_space=pl.ANY),
            *[pl.BlockSpec(memory_space=pltpu.VMEM) for _ in before],
        ],
        out_specs=[pl.BlockSpec(memory_space=pltpu.VMEM)] * 2,
        out_shape=[
            jax.ShapeDtypeStruct((rows, 2 * span, cols), jnp.bfloat16),
            jax.ShapeDtypeStruct(packed, jnp.float32),
        ],
        scratch_shapes=[
            pltpu.VMEM((2 * rows * span, half_lons), jnp.bfloat16),
            pltpu.VMEM(table.shape, table.dtype),
            pltpu.SemaphoreType.DMA((tiles,)),
            pltpu.VMEM(blocks.shape, blocks.dtype),
            pltpu.SemaphoreType.DMA((2,)),
        ],
        compiler_params=pltpu.CompilerParams(vmem_limit_bytes=VMEM_BYTES),
        cost_estimate=pl.CostEstimate(
            flops=8 * rows * span * half_lons * cols,
            bytes_accessed=2 * blocks.size + 4 * half_lons * cols + 4 * rows * span * cols,
            transcendentals=0,
        ),
    )(row_weight.reshape(1, -1), blocks, table, *before)


def dot_full(first, second, dims=(((1,), (0,)), ((), ()))):
    return lax.dot_general(
        first, second, dims, precision=highest, preferred_element_type=jnp.float32
    )


def eliminate(work, size, out_ref):
    height, width = work.shape
    for col in range(0, size, PIVOTS):
        base = col // 8 * 8
        lead = col - base
        rows = [work[lead + i : lead + i + 1, :] for i in range(PIVOTS)]
        cols = [
            jnp.broadcast_to(work[:, col + i : col + i + 1], (height - base, LANES)) for i in range(PIVOTS)
        ]
        update = None
        for i in range(PIVOTS):
            inverse = lax.rsqrt(cols[i][lead + i : lead + i + 1, :])
            wide = jnp.concatenate([inverse] * (width // LANES), axis=1)
            solved = rows[i] * wide
            out_ref[col + i : col + i + 1, :] = solved
            factor = cols[i] * inverse
            for k in range(i + 1, PIVOTS):
                share = factor[lead + k : lead + k + 1, :]
                cols[k] = cols[k] - factor * share
                rows[k] = rows[k] - solved * jnp.concatenate([share] * (width // LANES), axis=1)
            term = jnp.concatenate([factor] * (width // LANES), axis=1) * solved
            update = term if update is None else update + term
        following = (col + PIVOTS) // 8 * 8 - base
        work = work[following:] - update[following:]


def add_up(parts):
    while len(parts) > 1:
        parts = [parts[i] + parts[i + 1] for i in range(0, len(parts), 2)]
    return parts[0]


def merge_kernel(*refs, split):
    *part_refs, test_ref, early_ref, late_ref, out_ref, mix_ref, first_ref, second_ref, held, sems = refs
    rank = test_ref.shape[0]
    row = pl.program_id(0)
    fetches = [
        pltpu.make_async_copy(early_ref, held.at[pl.ds(0, split)], sems.at[0]),
        pltpu.make_async_copy(late_ref, held.at[pl.ds(split, late_ref.shape[0])], sems.at[1]),
    ]

    @pl.when(row == 0)
    def _():
        for fetch in fetches:
            fetch.start()
        gram = unpacked_gram(add_up([part[...] for part in part_refs]))
        test_t = test_ref[...]
        sketch = dot_full(gram, test_t, NT_DIMS)
        sketch_t = dot_full(test_t, gram)
        sketch_gram = dot_full(sketch_t, gram)
        power = dot_full(sketch_gram, sketch)
        power = 0.5 * (power + power.T)
        pad = jnp.zeros_like(power)
        eliminate(jnp.concatenate([power, pad, sketch_gram, sketch_t], axis=1), rank, first_ref)
        projected = first_ref[:, 2 * rank : 4 * rank]
        unmixed = first_ref[:, 4 * rank : 6 * rank]
        inner = dot_full(projected, projected, NT_DIMS)
        inner = 0.5 * (inner + inner.T)
        eliminate(jnp.concatenate([inner, pad], axis=1), rank, second_ref)
        upper = second_ref[:, :rank]
        row_ids, col_ids = ids(upper.shape)
        mixing = dot_full(jnp.where(col_ids >= row_ids, upper, 0.0), unmixed)
        top = mixing.astype(jnp.bfloat16)
        rest = (mixing - top.astype(jnp.float32)).astype(jnp.bfloat16)
        mix_ref[:rank, : 2 * rank] = top
        mix_ref[:rank, 2 * rank :] = top
        mix_ref[rank:, : 2 * rank] = rest
        mix_ref[rank:, 2 * rank :] = jnp.zeros_like(rest)

        for fetch in fetches:
            fetch.wait()

    cols = held.shape[2]
    for i in range(out_ref.shape[1] // cols):
        modes = held[row * (out_ref.shape[1] // cols) + i]
        both = jnp.dot(mix_ref[...], modes, preferred_element_type=jnp.float32)
        out_ref[:, i * cols : (i + 1) * cols] = both[:rank] + both[rank:]


def merge_and_mix(gram_parts, test_matrix, early, late):
    split, height, cols = early.shape
    rows = split + late.shape[0]
    some = rows if rows % 2 else rows // 2
    rank = test_matrix.shape[1]
    return pl.pallas_call(
        functools.partial(merge_kernel, split=split),
        grid=(rows // some,),
        in_specs=[
            *[pl.BlockSpec(part.shape, lambda i: (0, 0)) for part in gram_parts],
            pl.BlockSpec((rank, 2 * rank), lambda i: (0, 0)),
            pl.BlockSpec(memory_space=pl.ANY),
            pl.BlockSpec(memory_space=pl.ANY),
        ],
        out_specs=pl.BlockSpec((rank, some * cols), lambda i: (0, i)),
        out_shape=jax.ShapeDtypeStruct((rank, rows * cols), jnp.float32),
        scratch_shapes=[
            pltpu.VMEM((2 * rank, height), jnp.bfloat16),
            pltpu.VMEM((rank, 6 * rank), jnp.float32),
            pltpu.VMEM((rank, 2 * rank), jnp.float32),
            pltpu.VMEM((rows, height, cols), jnp.bfloat16),
            pltpu.SemaphoreType.DMA((2,)),
        ],
        compiler_params=pltpu.CompilerParams(vmem_limit_bytes=VMEM_BYTES),
    )(*gram_parts, test_matrix.T, early, late)


def exchanged(array, axes, bits):
    count = lax.axis_size(axes)
    masks = [0]
    for bit in bits:
        masks += [mask | bit for mask in masks]
    return [array] + [
        lax.ppermute(array, axes, [(i, i ^ mask) for i in range(count)]) for mask in masks[1:]
    ]


def sum_parts(array, axes):
    bits = [1 << k for k in range(lax.axis_size(axes).bit_length() - 1)]
    parts = exchanged(array, axes, bits[:1])
    for group in (bits[1:2] + bits[-1:], *[bits[k : k + 2] for k in range(2, len(bits) - 1, 2)]):
        parts = exchanged(add_up(parts), axes, group)
    return parts


def local_pair(snapshots, test_matrix):
    points, rank_rows, total_rows = snapshots.shape
    lon_count, group_count = lax.axis_size("lon"), lax.axis_size("tm")
    dev_rows = total_rows // (lon_count * group_count)
    first_row = (lax.axis_index("lon") * group_count + lax.axis_index("tm")) * dev_rows
    row_weight = area_weight(first_row, dev_rows, NTH)
    table = split_table(NPH, MMAX)
    split = EARLY_ROWS * dev_rows // 8
    early, late = relayout(snapshots, lon_count * group_count, split)
    late, table = lax.optimization_barrier((late, table))
    modes, gram = [], []
    for first, part in ((0, early), (split, late)):
        blocks = lax.all_to_all(part, ("lon", "tm"), split_axis=0, concat_axis=0, tiled=True)
        blocks = blocks.reshape(lon_count, group_count, -1, rank_rows, points)
        spectra, *gram = spectra_and_gram(blocks, row_weight, table, first, *gram)
        modes.append(spectra)
    return merge_and_mix(sum_parts(gram[0], ("tm", "lon")), test_matrix, *modes)


def solution(mesh):
    lon_count, group_count = mesh.shape["lon"], mesh.shape["tm"]
    device_count = lon_count * group_count
    whole_rows = NTH % device_count == 0 and NTH >= 2 * device_count
    whole_rows = whole_rows and device_count & (device_count - 1) == 0
    return jax.shard_map(
        local_pair if group_count == 2 and whole_rows else local_tree,
        mesh=mesh,
        in_specs=(P("lon", "tm", None), P()),
        out_specs=P(None, ("lon", "tm")),
        check_vma=False,
    )
```

```python
import functools
import math

import jax
import jax.numpy as jnp
from jax import lax
from jax.experimental import pallas as pl
from jax.experimental.pallas import tpu as pltpu
from jax.sharding import PartitionSpec as P

NPH = 2048
MMAX = 640
NTH = 256
COL_TILE = 256
LANES = 128
PIVOTS = 32
SNAPSHOT_TILE = 32
EARLY_ROWS = 6
VMEM_BYTES = 50 * 2**20
RELAYOUT_VMEM_BYTES = 58 * 2**20


highest = lax.Precision.HIGHEST
NT_DIMS = (((1,), (1,)), ((), ()))


def swapped(array, axis, distance):
    return lax.ppermute(array, axis, [(i, i ^ 1 << distance) for i in range(lax.axis_size(axis))])


def matmul(first_op, second_op):
    return jnp.dot(first_op, second_op, precision=highest, preferred_element_type=jnp.float32)


def spectral_table(points, wave_count, row_count):
    lon_ids = jnp.arange(row_count, dtype=jnp.int32)
    col_ids = jnp.arange(2 * wave_count, dtype=jnp.int32)
    wavenumber = jnp.where(col_ids < wave_count, col_ids, col_ids - wave_count + 1)
    phase_index = lon_ids[:, None] * wavenumber[None, :] % points
    angles = 2.0 * math.pi / points * phase_index.astype(jnp.float32)
    trig_value = jnp.where(col_ids[None, :] < wave_count, jnp.cos(angles), jnp.sin(angles))
    col_scale = math.sqrt(2.0 / points) / jnp.sqrt(
        1.0 + 4.0 * wavenumber.astype(jnp.float32) / wave_count
    )
    return trig_value * col_scale[None, :]


def area_weight(start_row, row_count, total_rows):
    row_ids = start_row + jnp.arange(row_count, dtype=jnp.int32)
    colatitude = math.pi * (row_ids.astype(jnp.float32) + 0.5) / (2.0 * total_rows)
    return jnp.sqrt(jnp.sin(colatitude))


def merge_gram(gram_matrix, test_matrix):
    sketch = matmul(gram_matrix, test_matrix)
    sketch_gram = matmul(sketch.T, gram_matrix)
    power_gram = matmul(sketch_gram, sketch)
    power_gram = 0.5 * (power_gram + power_gram.T)
    chol_first = jnp.linalg.cholesky(power_gram)
    projected = lax.linalg.triangular_solve(chol_first, sketch_gram, left_side=True, lower=True)
    proj_gram = matmul(projected, projected.T)
    chol_second = jnp.linalg.cholesky(0.5 * (proj_gram + proj_gram.T))
    unmixed = lax.linalg.triangular_solve(chol_first, sketch.T, left_side=True, lower=True)
    mixing = matmul(chol_second.T, unmixed)
    return (mixing, matmul(chol_second.T, chol_second))


def block_gram(low_energy, cross_term, high_energy):
    top_rows = jnp.concatenate([low_energy, cross_term], axis=1)
    bottom_rows = jnp.concatenate([cross_term.T, high_energy], axis=1)
    return jnp.concatenate([top_rows, bottom_rows], axis=0)


def combine_pair(mixing, low_modes, high_modes):
    rank_rows = low_modes.shape[0]
    return matmul(mixing[:, :rank_rows], low_modes) + matmul(mixing[:, rank_rows:], high_modes)


def own_columns(modes_flat, group_index, group_count):
    col_count = modes_flat.shape[1] // group_count
    return lax.dynamic_slice_in_dim(modes_flat, group_index * col_count, col_count, 1)


def local_tree(snapshots, test_matrix):
    dev_rows = NTH // lax.axis_size("lon")
    dft_table = spectral_table(NPH, MMAX, NPH)
    row_weight = area_weight(lax.axis_index("lon") * dev_rows, dev_rows, NTH)
    spectra = jnp.einsum(
        "pst,pk->stk",
        lax.all_to_all(snapshots, "lon", split_axis=2, concat_axis=0, tiled=True).astype(
            jnp.float32
        ),
        dft_table,
        precision=highest,
    )
    spectra = spectra * row_weight[None, :, None]
    rank_rows = spectra.shape[0]
    modes_now = spectra.reshape(rank_rows, -1)
    levels_count = lax.axis_size("tm").bit_length() - 1
    group_index = lax.axis_index("tm")
    group_count = lax.axis_size("tm")
    energy = lax.psum(matmul(modes_now, modes_now.T), "lon")
    start_level = 0
    for tree_level in range(start_level, levels_count):
        partner_modes, partner_energy = swapped((modes_now, energy), "tm", tree_level)
        is_upper = group_index // 2**tree_level % 2 == 1
        low_modes = jnp.where(is_upper, partner_modes, modes_now)
        high_modes = jnp.where(is_upper, modes_now, partner_modes)
        low_energy = jnp.where(is_upper, partner_energy, energy)
        high_energy = jnp.where(is_upper, energy, partner_energy)
        cross_term = lax.psum(matmul(low_modes, high_modes.T), "lon")
        mixing, energy = merge_gram(block_gram(low_energy, cross_term, high_energy), test_matrix)
        modes_now = combine_pair(mixing, low_modes, high_modes)
    return own_columns(modes_now, group_index, group_count)


def split_table(points, wave_count):
    table = spectral_table(points, wave_count, points // 2)
    table = table.reshape(points // 2, -1, COL_TILE).transpose(1, 0, 2)
    high = lax.reduce_precision(table, 8, 7)
    return jnp.stack([high.astype(jnp.bfloat16), (table - high).astype(jnp.bfloat16)], axis=1)


def ids(shape):
    return lax.broadcasted_iota(jnp.int32, shape, 0), lax.broadcasted_iota(jnp.int32, shape, 1)


def packed_gram(gram):
    rank = gram.shape[0] // 2
    high, cross, low = gram[:rank, :rank], gram[:rank, rank:], gram[rank:, rank:]
    row_ids, col_ids = ids(high.shape)
    both = jnp.where(col_ids >= row_ids, high, low)
    diagonal = jnp.sum(jnp.where(col_ids == row_ids, low, 0.0), axis=0, keepdims=True)
    diagonal = jnp.broadcast_to(jnp.concatenate([diagonal, diagonal], axis=1), (8, 2 * rank))
    return jnp.concatenate([jnp.concatenate([both, cross], axis=1), diagonal], axis=0)


def unpacked_gram(packed):
    rank = packed.shape[1] // 2
    both, cross, diagonal = packed[:rank, :rank], packed[:rank, rank:], packed[rank : rank + 1, :rank]
    row_ids, col_ids = ids(both.shape)
    turned = both.T
    high = jnp.where(col_ids >= row_ids, both, turned)
    low = jnp.where(col_ids < row_ids, both, turned)
    low = jnp.where(col_ids == row_ids, jnp.broadcast_to(diagonal, low.shape), low)
    top = jnp.concatenate([high, cross], axis=1)
    return jnp.concatenate([top, jnp.concatenate([cross.T, low], axis=1)], axis=0)


def relayout_kernel(x_ref, first_ref, last_ref):
    points, some, total = x_ref.shape
    devices, split = first_ref.shape[:2]
    by_snapshot = jnp.transpose(x_ref[...], (1, 0, 2))
    turned = jnp.stack([by_snapshot[i].T for i in range(some)], axis=0)
    rows = jnp.transpose(turned, (1, 0, 2)).reshape(devices, total // devices, some, points)
    first_ref[...] = rows[:, :split]
    last_ref[...] = rows[:, split:]


def relayout(snapshots, devices, split):
    points, rank_rows, total = snapshots.shape
    some = SNAPSHOT_TILE
    cuts = (split, total // devices - split)
    return pl.pallas_call(
        relayout_kernel,
        grid=(rank_rows // some,),
        in_specs=[pl.BlockSpec((points, some, total), lambda i: (0, i, 0))],
        out_specs=[pl.BlockSpec((devices, cut, some, points), lambda i: (0, 0, i, 0)) for cut in cuts],
        out_shape=[
            jax.ShapeDtypeStruct((devices, cut, rank_rows, points), snapshots.dtype) for cut in cuts
        ],
        compiler_params=pltpu.CompilerParams(vmem_limit_bytes=RELAYOUT_VMEM_BYTES),
    )(snapshots)


def spectra_kernel(*refs, first_row):
    weight_ref, x_ref, table_ref, *before, modes_ref, gram_ref, lhs, held, sems, own, own_sems = refs
    sources, groups, rows, rank_rows, points = x_ref.shape
    tiles = table_ref.shape[0]
    span = groups * rank_rows

    def fetch(step):
        return pltpu.make_async_copy(table_ref.at[step], held.at[step], sems.at[step])

    takes = []
    for half in range(2):
        part = pl.ds(half * sources // 2, sources // 2)
        takes.append(pltpu.make_async_copy(x_ref.at[part], own.at[part], own_sems.at[half]))
    for take in takes:
        take.start()
    fetch(0).start()
    for src in range(sources):
        half, place = divmod(src, sources // 2)
        if place == 0:
            takes[half].wait()
            for step in range(1 + half, tiles, 2):
                fetch(step).start()
        for row in range(rows):
            for grp in range(groups):
                start = ((half * rows + row) * groups + grp) * rank_rows
                lhs[start : start + rank_rows, place * points : (place + 1) * points] = own[
                    src, grp, row
                ]

    @pl.loop(0, tiles)
    def _(step):
        fetch(step).wait()
        tile = pl.ds(pl.multiple_of(step * COL_TILE, COL_TILE), COL_TILE)
        values = lhs[...]
        halves = jnp.dot(values, held[step, 0], preferred_element_type=jnp.float32)
        halves += jnp.dot(values, held[step, 1], preferred_element_type=jnp.float32)
        col_ids = step * COL_TILE + lax.broadcasted_iota(jnp.int32, (1, COL_TILE), 1)
        wavenumber = jnp.where(col_ids < MMAX, col_ids, col_ids - MMAX + 1)
        turned = (1 - 2 * (wavenumber & 1)).astype(jnp.float32)
        spectra = halves[: rows * span] + turned * halves[rows * span :]
        for row in range(rows):
            scaled = spectra[row * span : (row + 1) * span] * weight_ref[0, first_row + row]
            top = scaled.astype(jnp.bfloat16)
            rest = (scaled - top.astype(jnp.float32)).astype(jnp.bfloat16)
            modes_ref[row, :span, tile] = top
            modes_ref[row, span:, tile] = rest

    products = [
        lax.dot_general(
            modes_ref[row], modes_ref[row, :span, :], NT_DIMS, preferred_element_type=jnp.float32
        )
        for row in range(rows)
    ]
    total = functools.reduce(jnp.add, products)
    cross = total[span:]
    gram = total[:span] + (cross + cross.T)
    packed = packed_gram(gram)
    for ref in before:
        packed += ref[...]
    gram_ref[...] = packed


def spectra_and_gram(blocks, row_weight, table, first_row, *before):
    sources, groups, rows, rank_rows, points = blocks.shape
    tiles, _, half_lons, _ = table.shape
    cols = tiles * COL_TILE
    span = groups * rank_rows
    packed = (rank_rows + 8, span)
    return pl.pallas_call(
        functools.partial(spectra_kernel, first_row=first_row),
        in_specs=[
            pl.BlockSpec(memory_space=pltpu.SMEM),
            pl.BlockSpec(memory_space=pl.ANY),
            pl.BlockSpec(memory_space=pl.ANY),
            *[pl.BlockSpec(memory_space=pltpu.VMEM) for _ in before],
        ],
        out_specs=[pl.BlockSpec(memory_space=pltpu.VMEM)] * 2,
        out_shape=[
            jax.ShapeDtypeStruct((rows, 2 * span, cols), jnp.bfloat16),
            jax.ShapeDtypeStruct(packed, jnp.float32),
        ],
        scratch_shapes=[
            pltpu.VMEM((2 * rows * span, half_lons), jnp.bfloat16),
            pltpu.VMEM(table.shape, table.dtype),
            pltpu.SemaphoreType.DMA((tiles,)),
            pltpu.VMEM(blocks.shape, blocks.dtype),
            pltpu.SemaphoreType.DMA((2,)),
        ],
        compiler_params=pltpu.CompilerParams(vmem_limit_bytes=VMEM_BYTES),
        cost_estimate=pl.CostEstimate(
            flops=8 * rows * span * half_lons * cols,
            bytes_accessed=2 * blocks.size + 4 * half_lons * cols + 4 * rows * span * cols,
            transcendentals=0,
        ),
    )(row_weight.reshape(1, -1), blocks, table, *before)


def dot_full(first, second, dims=(((1,), (0,)), ((), ()))):
    return lax.dot_general(
        first, second, dims, precision=highest, preferred_element_type=jnp.float32
    )


def eliminate(work, size, out_ref):
    height, width = work.shape
    for col in range(0, size, PIVOTS):
        base = col // 8 * 8
        lead = col - base
        rows = [work[lead + i : lead + i + 1, :] for i in range(PIVOTS)]
        cols = [
            jnp.broadcast_to(work[:, col + i : col + i + 1], (height - base, LANES)) for i in range(PIVOTS)
        ]
        update = None
        for i in range(PIVOTS):
            inverse = lax.rsqrt(cols[i][lead + i : lead + i + 1, :])
            wide = jnp.concatenate([inverse] * (width // LANES), axis=1)
            solved = rows[i] * wide
            out_ref[col + i : col + i + 1, :] = solved
            factor = cols[i] * inverse
            for k in range(i + 1, PIVOTS):
                share = factor[lead + k : lead + k + 1, :]
                cols[k] = cols[k] - factor * share
                rows[k] = rows[k] - solved * jnp.concatenate([share] * (width // LANES), axis=1)
            term = jnp.concatenate([factor] * (width // LANES), axis=1) * solved
            update = term if update is None else update + term
        following = (col + PIVOTS) // 8 * 8 - base
        work = work[following:] - update[following:]


def add_up(parts):
    while len(parts) > 1:
        parts = [parts[i] + parts[i + 1] for i in range(0, len(parts), 2)]
    return parts[0]


def merge_kernel(*refs, split):
    *part_refs, test_ref, early_ref, late_ref, out_ref, mix_ref, first_ref, second_ref, held, sems = refs
    rank = test_ref.shape[0]
    row = pl.program_id(0)
    fetches = [
        pltpu.make_async_copy(early_ref, held.at[pl.ds(0, split)], sems.at[0]),
        pltpu.make_async_copy(late_ref, held.at[pl.ds(split, late_ref.shape[0])], sems.at[1]),
    ]

    @pl.when(row == 0)
    def _():
        for fetch in fetches:
            fetch.start()
        gram = unpacked_gram(add_up([part[...] for part in part_refs]))
        test_t = test_ref[...]
        sketch = dot_full(gram, test_t, NT_DIMS)
        sketch_t = dot_full(test_t, gram)
        sketch_gram = dot_full(sketch_t, gram)
        power = dot_full(sketch_gram, sketch)
        power = 0.5 * (power + power.T)
        pad = jnp.zeros_like(power)
        eliminate(jnp.concatenate([power, pad, sketch_gram, sketch_t], axis=1), rank, first_ref)
        projected = first_ref[:, 2 * rank : 4 * rank]
        unmixed = first_ref[:, 4 * rank : 6 * rank]
        inner = dot_full(projected, projected, NT_DIMS)
        inner = 0.5 * (inner + inner.T)
        eliminate(jnp.concatenate([inner, pad], axis=1), rank, second_ref)
        upper = second_ref[:, :rank]
        row_ids, col_ids = ids(upper.shape)
        mixing = dot_full(jnp.where(col_ids >= row_ids, upper, 0.0), unmixed)
        top = mixing.astype(jnp.bfloat16)
        rest = (mixing - top.astype(jnp.float32)).astype(jnp.bfloat16)
        mix_ref[:rank, : 2 * rank] = top
        mix_ref[:rank, 2 * rank :] = top
        mix_ref[rank:, : 2 * rank] = rest
        mix_ref[rank:, 2 * rank :] = jnp.zeros_like(rest)

        for fetch in fetches:
            fetch.wait()

    cols = held.shape[2]
    for i in range(out_ref.shape[1] // cols):
        modes = held[row * (out_ref.shape[1] // cols) + i]
        both = jnp.dot(mix_ref[...], modes, preferred_element_type=jnp.float32)
        out_ref[:, i * cols : (i + 1) * cols] = both[:rank] + both[rank:]


def merge_and_mix(gram_parts, test_matrix, early, late):
    split, height, cols = early.shape
    rows = split + late.shape[0]
    some = rows if rows % 2 else rows // 2
    rank = test_matrix.shape[1]
    return pl.pallas_call(
        functools.partial(merge_kernel, split=split),
        grid=(rows // some,),
        in_specs=[
            *[pl.BlockSpec(part.shape, lambda i: (0, 0)) for part in gram_parts],
            pl.BlockSpec((rank, 2 * rank), lambda i: (0, 0)),
            pl.BlockSpec(memory_space=pl.ANY),
            pl.BlockSpec(memory_space=pl.ANY),
        ],
        out_specs=pl.BlockSpec((rank, some * cols), lambda i: (0, i)),
        out_shape=jax.ShapeDtypeStruct((rank, rows * cols), jnp.float32),
        scratch_shapes=[
            pltpu.VMEM((2 * rank, height), jnp.bfloat16),
            pltpu.VMEM((rank, 6 * rank), jnp.float32),
            pltpu.VMEM((rank, 2 * rank), jnp.float32),
            pltpu.VMEM((rows, height, cols), jnp.bfloat16),
            pltpu.SemaphoreType.DMA((2,)),
        ],
        compiler_params=pltpu.CompilerParams(vmem_limit_bytes=VMEM_BYTES),
    )(*gram_parts, test_matrix.T, early, late)


def exchanged(array, axes, bits):
    count = lax.axis_size(axes)
    masks = [0]
    for bit in bits:
        masks += [mask | bit for mask in masks]
    return [array] + [
        lax.ppermute(array, axes, [(i, i ^ mask) for i in range(count)]) for mask in masks[1:]
    ]


def sum_parts(array, axes):
    bits = [1 << k for k in range(lax.axis_size(axes).bit_length() - 1)]
    parts = exchanged(array, axes, bits[:1])
    for group in (bits[1:2] + bits[-1:], *[bits[k : k + 2] for k in range(2, len(bits) - 1, 2)]):
        parts = exchanged(add_up(parts), axes, group)
    return parts


def local_pair(snapshots, test_matrix):
    points, rank_rows, total_rows = snapshots.shape
    lon_count, group_count = lax.axis_size("lon"), lax.axis_size("tm")
    dev_rows = total_rows // (lon_count * group_count)
    first_row = (lax.axis_index("lon") * group_count + lax.axis_index("tm")) * dev_rows
    row_weight = area_weight(first_row, dev_rows, NTH)
    table = split_table(NPH, MMAX)
    split = EARLY_ROWS * dev_rows // 8
    early, late = relayout(snapshots, lon_count * group_count, split)
    late, table = lax.optimization_barrier((late, table))
    modes, gram = [], []
    for first, part in ((0, early), (split, late)):
        blocks = lax.all_to_all(part, ("lon", "tm"), split_axis=0, concat_axis=0, tiled=True)
        blocks = blocks.reshape(lon_count, group_count, -1, rank_rows, points)
        spectra, *gram = spectra_and_gram(blocks, row_weight, table, first, *gram)
        modes.append(spectra)
    return merge_and_mix(sum_parts(gram[0], ("tm", "lon")), test_matrix, *modes)


def solution(mesh):
    lon_count, group_count = mesh.shape["lon"], mesh.shape["tm"]
    device_count = lon_count * group_count
    whole_rows = NTH % device_count == 0 and NTH >= 2 * device_count
    whole_rows = whole_rows and device_count & (device_count - 1) == 0
    return jax.shard_map(
        local_pair if group_count == 2 and whole_rows else local_tree,
        mesh=mesh,
        in_specs=(P("lon", "tm", None), P()),
        out_specs=P(None, ("lon", "tm")),
        check_vma=False,
    )
```
